32 devices in a mesh: groups: 2 (over y), fsdp: 4 (over z), dp: 4 (over x, core).
Axes of the slice: x: 2, y: 2, z: 4, core: 2. Of those that a mesh axis runs over, the one named last changes fastest.
Arguments:
- stats: bfloat16 [8, 8, 512, 512], P(('groups', 'dp'), None, 'fsdp'), parts along dimension 0, as said below
- grad: bfloat16 [8, 8, 512, 512], P(('groups', 'dp'), None, 'fsdp'), parts along dimension 0
- due: int32 [8, 8], P(('groups', 'dp')), parts along dimension 0, may hold values 0 or 1
- cost: int32 [8, 8], P(('groups', 'dp')), parts along dimension 0, may hold values from 1 to 4
- assign: int32 [8, 8], P(('groups', 'dp')), parts along dimension 0, may hold values from 0 to 7, each once within a row
- stale: bfloat16 [8, 8, 512, 512], P(('groups', 'dp'), 'fsdp'), parts along dimension 0, as said below
Outputs:
- update: bfloat16 [8, 8, 512, 512], P(('groups', 'dp'), None, 'fsdp'), parts along dimension 0
The draws below stay inside these ranges and needn't reach their ends.
There are 2 independent parts, one for each index of `groups`. The reference program is written for one: setup_inputs(seed, part) draws one part's arguments, and reference() takes and returns one part's arrays. A program takes and returns all parts, laid end to end along the dimension named above; each array names one. Nothing has to cross between parts.
Inputs may be any that keep to these rules, and one draw needn't show every extreme that they name: Each dp index's row of assign is a permutation of the 8 solver slots; slot q belongs to the solver at fsdp index q // 2, and stale[d, q] is the previous root held in that slot. `stats`: every block is symmetric positive definite. `stale`: every block is symmetric positive definite.
All inputs are finite; a program needn't handle non-finite values. No bound on the sum of `due` on one device may be relied on, other than what follows from the above.
Results may differ from the reference program's by a relative error of at most 0.0009.
The reference program's roundings to bfloat16 on the way count: a program that leaves them out, or rounds other values in their place, can miss the bound.
Values may be sent and summed in bfloat16 or wider, within the bound.
No kernel may reach another device: no remote copies, remote signals or barrier semaphores. Data moves between devices by JAX's collectives and lax.ppermute only.
A program may use at most 64 MiB of HBM per device.

```python
import jax
import jax.numpy as jnp
from jax import lax

BLOCK = 512
GC = 512
ITERS = 4
ROWBLK = 8
NBLK = 32
N_DP = 4


def mixed_blocks(key, block_total, block_order, scale_top, coupling):
    key_scale, key_core = jax.random.split(key)
    scales = jnp.exp(0.5 * jnp.log(scale_top) * jax.random.uniform(key_scale, (block_total, block_order), jnp.float32))
    half_width = coupling * (6.0 / block_order) ** 0.5
    raw_noise = jax.random.uniform(key_core, (block_total, block_order, block_order), jnp.float32, -half_width, half_width)
    symmetric = 0.5 * (raw_noise + jnp.swapaxes(raw_noise, 1, 2))
    identity = jnp.eye(block_order, dtype=jnp.float32)
    core_matrix = identity + symmetric * (1.0 - identity)
    return core_matrix * scales[:, :, None] * scales[:, None, :]


def kernel_blocks(key, block_total, block_order, scale_top):
    key_spread, key_points = jax.random.split(key)
    row_index = jnp.arange(block_order, dtype=jnp.float32)
    rising = jnp.exp(0.5 * jnp.log(3.0) * row_index / max(block_order - 1, 1))
    spread = jnp.exp(0.5 * jnp.log(scale_top) * jax.random.uniform(key_spread, (block_total, block_order), jnp.float32))
    scales = spread * rising[None, :]
    points = jax.random.uniform(key_points, (block_total, block_order), jnp.float32)
    correlation = 1.0 - 4.0 / block_order
    distance = jnp.abs(row_index[:, None] - row_index[None, :])
    banded = jnp.exp(distance * jnp.log(correlation))
    mixing = jnp.exp(-jnp.abs(points[:, :, None] - points[:, None, :]))
    identity = jnp.eye(block_order, dtype=jnp.float32)
    core_matrix = banded[None, :, :] * mixing + 0.5 * identity[None, :, :]
    return core_matrix * scales[:, :, None] * scales[:, None, :]


def draw_stats(key, part):
    key = jax.random.fold_in(key, 11)
    scale_top = 10.0
    blocks = kernel_blocks(key, NBLK, BLOCK, scale_top)
    return blocks.reshape(NBLK // ROWBLK, ROWBLK, BLOCK, BLOCK).astype(jnp.bfloat16)


def draw_stale(key, part):
    key = jax.random.fold_in(key, 23)
    blocks = BLOCK ** (-0.5) * mixed_blocks(key, NBLK, BLOCK, 4.0, 0.3)
    return blocks.reshape(NBLK // ROWBLK, ROWBLK, BLOCK, BLOCK).astype(jnp.bfloat16)


def draw_grad(key, part):
    key = jax.random.fold_in(key, 37)
    key_noise = jax.random.fold_in(key, 0)
    key_rows = jax.random.fold_in(key, 1)
    key_cols = jax.random.fold_in(key, 2)
    key_lift = jax.random.fold_in(key, 4)
    key_weight = jax.random.fold_in(key, 5)
    full_shape = (NBLK, BLOCK, GC)
    base_noise = jax.random.normal(key_noise, full_shape, jnp.float32)
    scale_top = 10.0
    amplitude = 4.5
    row_scale = jnp.exp(jnp.log(scale_top) * jax.random.uniform(key_rows, (NBLK, BLOCK, 1), jnp.float32))
    column_scale = jnp.exp(jnp.log(scale_top) * jax.random.uniform(key_cols, (1, 1, GC), jnp.float32))
    row_lift = jax.random.uniform(key_lift, (NBLK, BLOCK, 1), jnp.float32, 0.5, 1.5)
    col_weight = jax.random.normal(key_weight, (NBLK, 1, GC), jnp.float32)
    common = amplitude * row_lift * col_weight
    rise_factor = jnp.exp(0.5 * jnp.log(3.0) * jnp.arange(NBLK, dtype=jnp.float32) / max(NBLK - 1, 1))
    values = (base_noise * row_scale + common) * column_scale * rise_factor[:, None, None]
    return values.reshape(NBLK // ROWBLK, ROWBLK, BLOCK, GC).astype(jnp.bfloat16)


def plant(entries, key, smallest, largest):
    index_at = [jax.random.randint(jax.random.fold_in(key, axis), (), 0, length) for axis, length in enumerate(entries.shape)]
    main_axis = entries.shape.index(max(entries.shape))
    beside = index_at[:main_axis] + [(index_at[main_axis] + 1) % entries.shape[main_axis]] + index_at[main_axis + 1:]
    return entries.at[tuple(index_at)].set(smallest).at[tuple(beside)].set(largest)


def setup_inputs(seed: int = 0, part: int = 0) -> dict:
    streams_of = jax.random.split(jax.random.key(seed), 7)
    own_keys = jax.random.split(jax.random.fold_in(streams_of[6], part), 7)
    return {
        "stats": draw_stats(jax.random.fold_in(jax.random.fold_in(streams_of[6], part), 71), part),
        "grad": draw_grad(jax.random.fold_in(jax.random.fold_in(streams_of[6], part), 71), part),
        "due": plant((jax.random.randint(own_keys[2], (N_DP, ROWBLK), 0, 2) < 1).astype(jnp.int32), jax.random.fold_in(own_keys[2], 1), 0, 1),
        "cost": plant(jax.random.randint(own_keys[3], (N_DP, ROWBLK), 1, ITERS + 1), jax.random.fold_in(own_keys[3], 1), 1, ITERS).astype(jnp.int32),
        "assign": jax.vmap(lambda own: jax.random.permutation(own, ROWBLK))(jax.random.split(own_keys[4], N_DP)).reshape((N_DP, ROWBLK)).astype(jnp.int32),
        "stale": draw_stale(jax.random.fold_in(jax.random.fold_in(streams_of[6], part), 71), part),
    }


KL_BOUND = 1.0

def refresh(block_piece, grad_rows, old_root, due_flag, sweep_count):
    full_block = block_piece.astype(jnp.float32)
    frobenius = jnp.sqrt(jnp.sum(full_block * full_block))
    identity = jnp.eye(full_block.shape[0], dtype=jnp.float32)
    root_half = (full_block / frobenius).astype(jnp.bfloat16)
    root_inverse = identity.astype(jnp.bfloat16)

    def sweep(step_index, iterates):
        half_now, inverse_now = iterates
        product = jnp.dot(inverse_now, half_now, preferred_element_type=jnp.float32)
        correction = (1.5 * identity - 0.5 * product).astype(jnp.bfloat16)
        half_next = jnp.dot(half_now, correction, preferred_element_type=jnp.float32).astype(jnp.bfloat16)
        inverse_next = jnp.dot(correction, inverse_now, preferred_element_type=jnp.float32).astype(jnp.bfloat16)
        return (half_next, inverse_next)
    root_half, root_inverse = lax.fori_loop(0, sweep_count, sweep, (root_half, root_inverse))
    left_factor = jnp.where(due_flag > 0, root_inverse, old_root)
    factor = jnp.where(due_flag > 0, lax.rsqrt(frobenius), jnp.float32(1.0))
    return (jnp.dot(left_factor, grad_rows, preferred_element_type=jnp.float32) * factor).astype(jnp.bfloat16)

def reference(stats, grad, due, cost, assign, stale):
    dp_count, block_count = assign.shape
    block_order = stats.shape[2]
    column_count = grad.shape[3]
    chosen = jax.vmap(lambda store, index_row: jnp.take(store, index_row, axis=0))(stale, assign)
    flattened = (stats.reshape(-1, block_order, block_order), grad.reshape(-1, block_order, column_count), chosen.reshape(-1, block_order, block_order), due.reshape(-1), (cost * due).reshape(-1))
    solved = lax.map(lambda items: refresh(*items), flattened)
    quadratic = jnp.sum(solved.astype(jnp.float32) * grad.reshape(-1, block_order, column_count).astype(jnp.float32))
    elements = dp_count * block_count * block_order * column_count
    clip_factor = jnp.minimum(jnp.float32(1.0), jnp.sqrt(KL_BOUND * elements / quadratic))
    return (clip_factor * solved.astype(jnp.float32)).astype(jnp.bfloat16).reshape(grad.shape)
```

```python
import functools

import jax
import jax.numpy as jnp
from jax import lax
from jax.experimental import pallas as pl
from jax.experimental.pallas import tpu as pltpu
from jax.sharding import PartitionSpec as P

KL_BOUND = 1.0
VMEM_BYTES = 40 * 2**20
F32 = jnp.float32
BF16 = jnp.bfloat16


def refresh(block_piece, grad_rows, old_root, due_flag, sweep_count):
    full_block = block_piece.astype(F32)
    frobenius = jnp.sqrt(jnp.sum(full_block * full_block))
    identity = jnp.eye(full_block.shape[0], dtype=F32)
    root_half = (full_block / frobenius).astype(BF16)
    root_inverse = identity.astype(BF16)

    def sweep(step_index, iterates):
        half_now, inverse_now = iterates
        product = jnp.dot(inverse_now, half_now, preferred_element_type=F32)
        correction = (1.5 * identity - 0.5 * product).astype(BF16)
        half_next = jnp.dot(half_now, correction, preferred_element_type=F32).astype(BF16)
        inverse_next = jnp.dot(correction, inverse_now, preferred_element_type=F32).astype(BF16)
        return (half_next, inverse_next)

    root_half, root_inverse = lax.fori_loop(0, sweep_count, sweep, (root_half, root_inverse))
    left_factor = jnp.where(due_flag > 0, root_inverse, old_root)
    factor = jnp.where(due_flag > 0, lax.rsqrt(frobenius), F32(1.0))
    return (jnp.dot(left_factor, grad_rows, preferred_element_type=F32) * factor).astype(BF16)


def exchange_all(stats, grad, due, cost, assign, stale):
    own_index = lax.axis_index("fsdp")
    solver_count = lax.axis_size("fsdp")
    dp_count = lax.axis_size("dp")
    table_row = assign[0]
    due_row = due[0]
    cost_row = cost[0]
    total_slots = table_row.shape[0]
    slot_count = total_slots // solver_count
    row_count = stats.shape[2]
    block_order = stats.shape[3]
    column_count = grad.shape[3]
    source = jnp.argsort(table_row, stable=True)
    sent_stats = jnp.take(stats[0], source, axis=0).reshape(
        solver_count, slot_count, row_count, block_order
    )
    sent_grad = jnp.take(grad[0], source, axis=0).reshape(
        solver_count, slot_count, row_count, column_count
    )
    blocks_here, grads_here = (
        lax.all_to_all(sent_stats, "fsdp", split_axis=0, concat_axis=2, tiled=True),
        lax.all_to_all(sent_grad, "fsdp", split_axis=0, concat_axis=2, tiled=True),
    )
    my_blocks = lax.dynamic_slice_in_dim(source, own_index * slot_count, slot_count)
    results = []
    for slot in range(slot_count):
        block_id = my_blocks[slot]
        due_flag = due_row[block_id]
        results.append(
            refresh(
                blocks_here[0, slot],
                grads_here[0, slot],
                stale[0, slot],
                due_flag,
                cost_row[block_id] * due_flag,
            )
        )
    solved = jnp.stack(results)
    returned = lax.all_to_all(
        solved.reshape(slot_count, solver_count, row_count, column_count),
        "fsdp",
        split_axis=1,
        concat_axis=0,
        tiled=True,
    )
    owner_rows = jnp.take(returned.reshape(total_slots, row_count, column_count), table_row, axis=0)
    local_part = jnp.sum(owner_rows.astype(F32) * grad[0].astype(F32))
    quadratic = lax.psum(local_part, ("fsdp", "dp"))
    elements = dp_count * total_slots * block_order * column_count
    clip_factor = jnp.minimum(F32(1.0), jnp.sqrt(KL_BOUND * elements / quadratic))
    return (clip_factor * owner_rows.astype(F32)).astype(BF16)[None]


def call(kernel, out_shape, in_specs, out_specs, name, scratch=(), flops=0, moved=0):
    return pl.pallas_call(
        kernel,
        out_shape=out_shape,
        in_specs=in_specs,
        out_specs=out_specs,
        scratch_shapes=list(scratch),
        compiler_params=pltpu.CompilerParams(vmem_limit_bytes=VMEM_BYTES),
        cost_estimate=pl.CostEstimate(flops=flops, bytes_accessed=moved, transcendentals=0),
        name=name,
    )


IN_VMEM = pl.BlockSpec(memory_space=pltpu.VMEM)
IN_SMEM = pl.BlockSpec(memory_space=pltpu.SMEM)
ANYWHERE = pl.BlockSpec(memory_space=pl.ANY)


def block_in_slot(assign_ref, slot):
    found = jnp.int32(0)
    for block in range(assign_ref.shape[1]):
        found = jnp.where(assign_ref[0, block] == slot, jnp.int32(block), found)
    return found


def tile_at(index, width):
    return pl.ds(pl.multiple_of(index * width, width), width)


def pack_stats_kernel(slots, me_ref, assign_ref, stats_ref, near_ref, far2_ref, far3_ref):
    me = me_ref[0]
    width = stats_ref.shape[2]
    half = width // 2
    odd = me % 2
    for slot in range(slots):
        for far, out in ((2, far2_ref), (3, far3_ref)):
            block = block_in_slot(assign_ref, (me ^ far) * slots + slot)
            out[slot, :width, :] = stats_ref[0, block, :, tile_at(me, width)]
            between = stats_ref[0, block, :, tile_at(me ^ 1, width)].astype(F32)
            out[slot, width:, :] = jnp.where(
                odd == 1, between.T[half:, :], between[:half, :]
            ).astype(BF16)
    for slot in range(slots):
        block = block_in_slot(assign_ref, (me ^ 1) * slots + slot)
        for place, other in enumerate((0, 2, 3)):
            near_ref[slot, :, place * width : (place + 1) * width] = stats_ref[
                0, block, :, tile_at(me ^ other, width)
            ]


def pack_stats(me, assign, stats, slots):
    width, order = stats.shape[2:]
    near = jax.ShapeDtypeStruct((slots, width, order - width), BF16)
    far = jax.ShapeDtypeStruct((slots, width + width // 2, width), BF16)
    return call(
        functools.partial(pack_stats_kernel, slots),
        (near, far, far),
        [IN_SMEM, IN_SMEM, IN_VMEM],
        (IN_VMEM,) * 3,
        "pack_stats",
        moved=2 * stats.size * 2,
    )(me, assign, stats)


def pack_grad_kernel(slots, me_ref, assign_ref, grad_ref, *rest):
    outs, sems = rest[:-1], rest[-1]
    me = me_ref[0]
    copies = []
    for slot in range(slots):
        for far in range(4):
            at = slot * 4 + far
            block = block_in_slot(assign_ref, (me ^ far) * slots + slot)
            copy = pltpu.make_async_copy(grad_ref.at[0, block], outs[at], sems.at[at])
            copy.start()
            copies.append(copy)
    for copy in copies:
        copy.wait()


def pack_grad(me, assign, grad, slots):
    out = jax.ShapeDtypeStruct(grad.shape[2:], BF16)
    count = 4 * slots
    flat = call(
        functools.partial(pack_grad_kernel, slots),
        (out,) * count,
        [IN_SMEM, IN_SMEM, ANYWHERE],
        (ANYWHERE,) * count,
        "pack_grad",
        scratch=[pltpu.SemaphoreType.DMA((count,))],
        moved=2 * grad.size * 2,
    )(me, assign, grad)
    return [flat[slot * 4 : slot * 4 + 4] for slot in range(slots)]


def root_kernel(
    slots,
    me_ref,
    assign_ref,
    due_ref,
    cost_ref,
    stats_ref,
    near_ref,
    far2_ref,
    far3_ref,
    stale_ref,
    root_ref,
    factor_ref,
    own,
    full,
    half_root,
    correction,
    sem,
    stale_sem,
):
    me = me_ref[0]
    order = full.shape[0]
    width = near_ref.shape[1]
    half = width // 2
    chunk = order // 2
    rows = [pl.ds(start, chunk) for start in range(0, order, chunk)]

    def eye_rows(start):
        r = lax.broadcasted_iota(jnp.int32, (chunk, order), 0) + start
        c = lax.broadcasted_iota(jnp.int32, (chunk, order), 1)
        return jnp.where(r == c, F32(1.5), F32(0.0))

    def assemble(slot, block):
        copy = pltpu.make_async_copy(stats_ref.at[0, block], own, sem)
        copy.start()
        even, odd = (me ^ 2) & 2, ((me ^ 2) & 2) + 1
        at = lambda index: tile_at(index, width)
        two, three = me ^ 2, me ^ 3
        full[at(two), at(two)] = far2_ref[slot, :width, :].astype(F32)
        full[at(three), at(three)] = far3_ref[slot, :width, :].astype(F32)
        from_two = far2_ref[slot, width:, :].astype(F32)
        from_three = far3_ref[slot, width:, :].astype(F32)
        two_is_even = me % 2 == 0
        between = jnp.concatenate(
            [
                jnp.where(two_is_even, from_two, from_three),
                jnp.where(two_is_even, from_three, from_two),
            ],
            axis=0,
        )
        full[at(even), at(odd)] = between
        full[at(odd), at(even)] = between.T
        near = me ^ 1
        for place, other in enumerate((0, 2, 3)):
            tile = near_ref[slot, :, place * width : (place + 1) * width].astype(F32)
            full[at(near), at(near ^ other)] = tile
            if other:
                full[at(near ^ other), at(near)] = tile.T
        copy.wait()
        full[at(me), :] = own[...].astype(F32)
        for other in (1, 2, 3):
            full[at(me ^ other), at(me)] = own[:, at(me ^ other)].astype(F32).T

    for slot in range(slots):
        block = block_in_slot(assign_ref, me * slots + slot)
        due = due_ref[0, block]
        cost = cost_ref[0, block]
        factor_ref[slot] = F32(1.0)

        @pl.when(due <= 0)
        def _():
            copy = pltpu.make_async_copy(stale_ref.at[0, slot], root_ref.at[slot], stale_sem)
            copy.start()
            copy.wait()

        @pl.when(due > 0)
        def _():
            assemble(slot, block)
            total = jnp.zeros((8, order), F32)
            for start in range(0, order, 8):
                piece = full[start : start + 8, :]
                total = total + piece * piece
            norm = jnp.sqrt(jnp.full((8, 128), jnp.sum(total), F32))
            factor_ref[slot] = lax.rsqrt(norm)[0, 0]
            divisor = jnp.max(norm)
            for i, start in enumerate(range(0, order, chunk)):
                scaled = (full[rows[i], :] / divisor).astype(BF16)
                half_root[rows[i], :] = scaled
                root_ref[slot, rows[i], :] = (eye_rows(start) - 0.5 * scaled.astype(F32)).astype(
                    BF16
                )

            @pl.when(cost > 1)
            def _():
                first = [
                    jnp.dot(half_root[r, :], root_ref[slot], preferred_element_type=F32).astype(BF16)
                    for r in rows
                ]
                for r, value in zip(rows, first):
                    half_root[r, :] = value

                def correct():
                    for i, start in enumerate(range(0, order, chunk)):
                        product = jnp.dot(
                            root_ref[slot, rows[i], :], half_root[...], preferred_element_type=F32
                        )
                        correction[rows[i], :] = (eye_rows(start) - 0.5 * product).astype(BF16)

                def next_root():
                    values = [
                        jnp.dot(
                            correction[r, :], root_ref[slot], preferred_element_type=F32
                        ).astype(BF16)
                        for r in rows
                    ]
                    for r, value in zip(rows, values):
                        root_ref[slot, r, :] = value

                def sweep(step, carry):
                    correct()
                    values = [
                        jnp.dot(
                            half_root[r, :], correction[...], preferred_element_type=F32
                        ).astype(BF16)
                        for r in rows
                    ]
                    for r, value in zip(rows, values):
                        half_root[r, :] = value
                    next_root()
                    return carry

                lax.fori_loop(0, cost - 2, sweep, 0)
                correct()
                next_root()


def roots(me, assign, due, cost, stats, received, stale, slots):
    order = stats.shape[3]
    width = stats.shape[2]
    return call(
        functools.partial(root_kernel, slots),
        (
            jax.ShapeDtypeStruct((slots, order, order), BF16),
            jax.ShapeDtypeStruct((slots,), F32),
        ),
        [IN_SMEM] * 4 + [ANYWHERE] + [IN_VMEM] * 3 + [ANYWHERE],
        (IN_VMEM, IN_SMEM),
        "roots",
        scratch=[
            pltpu.VMEM((width, order), BF16),
            pltpu.VMEM((order, order), F32),
            pltpu.VMEM((order, order), BF16),
            pltpu.VMEM((order, order), BF16),
            pltpu.SemaphoreType.DMA,
            pltpu.SemaphoreType.DMA,
        ],
        flops=slots * 9 * 2 * order**3,
        moved=slots * order * order * 6,
    )(me, assign, due, cost, stats, *received, stale)


def product_kernel(slot, me_ref, root_ref, factor_ref, *rest):
    sum_in_ref = rest[0] if slot else None
    pieces = rest[1 if slot else 0 :][:4]
    outs = rest[-6:-2]
    sum_ref, whole = rest[-2:]
    me = me_ref[0]
    width = pieces[0].shape[0]
    for far in range(4):
        whole[tile_at(me ^ far, width), :] = pieces[far][...]
    total = sum_in_ref[...] if slot else jnp.zeros(sum_ref.shape, F32)
    for far in (2, 3, 1, 0):
        piece = jnp.dot(
            root_ref[slot, tile_at(me ^ far, width), :], whole[...], preferred_element_type=F32
        )
        rounded = (piece * factor_ref[slot]).astype(BF16)
        outs[far][...] = rounded
        terms = rounded.astype(F32) * pieces[far][...].astype(F32)
        for start in range(0, width, 8):
            for column in range(0, terms.shape[1], 128):
                total = total + terms[start : start + 8, column : column + 128]
    sum_ref[...] = total


def product(slot, me, root, factor, pieces, so_far):
    width, columns = pieces[0].shape
    order = root.shape[1]
    before = [] if so_far is None else [so_far]
    *rows, total = call(
        functools.partial(product_kernel, slot),
        (jax.ShapeDtypeStruct((width, columns), BF16),) * 4
        + (jax.ShapeDtypeStruct((8, 128), F32),),
        [IN_SMEM, IN_VMEM, IN_SMEM] + [IN_VMEM] * (len(before) + 4),
        (IN_VMEM,) * 5,
        "product",
        scratch=[pltpu.VMEM((order, columns), BF16)],
        flops=2 * order * order * columns,
        moved=3 * order * order * 2,
    )(me, root, factor, *before, *pieces)
    return rows, total


def clip_kernel(slots, elements, me_ref, assign_ref, *rest):
    sums, rows, out_ref = rest[:4], rest[4:-1], rest[-1]
    me = me_ref[0]
    quadratic = jnp.sum(sums[0][...] + sums[1][...] + sums[2][...] + sums[3][...])
    ratio = jnp.full((8, 128), F32(KL_BOUND * elements)) / quadratic
    clip_factor = jnp.max(jnp.minimum(F32(1.0), jnp.sqrt(ratio)))
    for slot in range(slots):
        for far in range(4):
            block = block_in_slot(assign_ref, (me ^ far) * slots + slot)
            out_ref[0, block] = (clip_factor * rows[slot * 4 + far][...].astype(F32)).astype(BF16)


def clip(me, assign, sums, rows, shape, slots, elements):
    return call(
        functools.partial(clip_kernel, slots, elements),
        jax.ShapeDtypeStruct(shape, BF16),
        [IN_SMEM, IN_SMEM] + [IN_VMEM] * (len(sums) + len(rows)),
        IN_VMEM,
        "clip",
        moved=4 * shape[1] * shape[2] * shape[3],
    )(me, assign, *sums, *rows)


def partner_of(value, axis, far):
    count = lax.axis_size(axis)
    return lax.ppermute(value, axis, [(i, i ^ far) for i in range(count)])


def sum_over(value, axis):
    count = lax.axis_size(axis)
    total = value
    for shift in range(1, count):
        total = total + lax.ppermute(
            value, axis, [(i, (i + shift) % count) for i in range(count)]
        )
    return total


def exchange_four(stats, grad, due, cost, assign, stale):
    me = lax.axis_index("fsdp").astype(jnp.int32).reshape(1)
    slots = assign.shape[1] // 4
    near, far2, far3 = pack_stats(me, assign, stats, slots)
    received = [None] * 3
    received[1] = partner_of(far2, "fsdp", 2)
    received[2] = partner_of(far3, "fsdp", 3)
    received[0] = partner_of(near, "fsdp", 1)
    sent = pack_grad(me, assign, grad, slots)
    pieces = []
    for slot in range(slots):
        here = {0: sent[slot][0]}
        for far in (3, 2, 1):
            here[far] = partner_of(sent[slot][far], "fsdp", far)
        pieces.append([here[far] for far in range(4)])
    root, factor = roots(me, assign, due, cost, stats, received, stale, slots)
    rows, total = [], None
    for slot in range(slots):
        solved, total = product(slot, me, root, factor, pieces[slot], total)
        back = {0: solved[0]}
        for far in (3, 2, 1):
            back[far] = partner_of(solved[far], "fsdp", far)
        rows += [back[far] for far in range(4)]
    total = sum_over(total, "dp")
    sums = [total] + [partner_of(total, "fsdp", far) for far in (1, 2, 3)]
    elements = lax.axis_size("dp") * assign.shape[1] * stats.shape[3] * grad.shape[3]
    return clip(me, assign, sums, rows, grad.shape, slots, elements)


def solution(mesh):
    return jax.shard_map(
        exchange_four if mesh.shape["fsdp"] == 4 else exchange_all,
        mesh=mesh,
        in_specs=(
            P(("groups", "dp"), None, "fsdp", None),
            P(("groups", "dp"), None, "fsdp", None),
            P(("groups", "dp"), None),
            P(("groups", "dp"), None),
            P(("groups", "dp"), None),
            P(("groups", "dp"), "fsdp", None, None),
        ),
        out_specs=P(("groups", "dp"), None, "fsdp", None),
        check_vma=False,
    )
```

```python
import functools

import jax
import jax.numpy as jnp
from jax import lax
from jax.experimental import pallas as pl
from jax.experimental.pallas import tpu as pltpu
from jax.sharding import PartitionSpec as P

KL_BOUND = 1.0
VMEM_BYTES = 40 * 2**20
DIAGONAL_ROWS = 16
F32 = jnp.float32
BF16 = jnp.bfloat16


def refresh(block_piece, grad_rows, old_root, due_flag, sweep_count):
    full_block = block_piece.astype(F32)
    frobenius = jnp.sqrt(jnp.sum(full_block * full_block))
    identity = jnp.eye(full_block.shape[0], dtype=F32)
    root_half = (full_block / frobenius).astype(BF16)
    root_inverse = identity.astype(BF16)

    def sweep(step_index, iterates):
        half_now, inverse_now = iterates
        product = jnp.dot(inverse_now, half_now, preferred_element_type=F32)
        correction = (1.5 * identity - 0.5 * product).astype(BF16)
        half_next = jnp.dot(half_now, correction, preferred_element_type=F32).astype(BF16)
        inverse_next = jnp.dot(correction, inverse_now, preferred_element_type=F32).astype(BF16)
        return (half_next, inverse_next)

    root_half, root_inverse = lax.fori_loop(0, sweep_count, sweep, (root_half, root_inverse))
    left_factor = jnp.where(due_flag > 0, root_inverse, old_root)
    factor = jnp.where(due_flag > 0, lax.rsqrt(frobenius), F32(1.0))
    return (jnp.dot(left_factor, grad_rows, preferred_element_type=F32) * factor).astype(BF16)


def exchange_all(stats, grad, due, cost, assign, stale):
    own_index = lax.axis_index("fsdp")
    solver_count = lax.axis_size("fsdp")
    dp_count = lax.axis_size("dp")
    table_row = assign[0]
    due_row = due[0]
    cost_row = cost[0]
    total_slots = table_row.shape[0]
    slot_count = total_slots // solver_count
    row_count = stats.shape[2]
    block_order = stats.shape[3]
    column_count = grad.shape[3]
    source = jnp.argsort(table_row, stable=True)
    sent_stats = jnp.take(stats[0], source, axis=0).reshape(
        solver_count, slot_count, row_count, block_order
    )
    sent_grad = jnp.take(grad[0], source, axis=0).reshape(
        solver_count, slot_count, row_count, column_count
    )
    blocks_here, grads_here = (
        lax.all_to_all(sent_stats, "fsdp", split_axis=0, concat_axis=2, tiled=True),
        lax.all_to_all(sent_grad, "fsdp", split_axis=0, concat_axis=2, tiled=True),
    )
    my_blocks = lax.dynamic_slice_in_dim(source, own_index * slot_count, slot_count)
    results = []
    for slot in range(slot_count):
        block_id = my_blocks[slot]
        due_flag = due_row[block_id]
        results.append(
            refresh(
                blocks_here[0, slot],
                grads_here[0, slot],
                stale[0, slot],
                due_flag,
                cost_row[block_id] * due_flag,
            )
        )
    solved = jnp.stack(results)
    returned = lax.all_to_all(
        solved.reshape(slot_count, solver_count, row_count, column_count),
        "fsdp",
        split_axis=1,
        concat_axis=0,
        tiled=True,
    )
    owner_rows = jnp.take(returned.reshape(total_slots, row_count, column_count), table_row, axis=0)
    local_part = jnp.sum(owner_rows.astype(F32) * grad[0].astype(F32))
    quadratic = lax.psum(local_part, ("fsdp", "dp"))
    elements = dp_count * total_slots * block_order * column_count
    clip_factor = jnp.minimum(F32(1.0), jnp.sqrt(KL_BOUND * elements / quadratic))
    return (clip_factor * owner_rows.astype(F32)).astype(BF16)[None]


def call(kernel, out_shape, in_specs, out_specs, name, scratch=(), flops=0, moved=0):
    return pl.pallas_call(
        kernel,
        out_shape=out_shape,
        in_specs=in_specs,
        out_specs=out_specs,
        scratch_shapes=list(scratch),
        compiler_params=pltpu.CompilerParams(vmem_limit_bytes=VMEM_BYTES),
        cost_estimate=pl.CostEstimate(flops=flops, bytes_accessed=moved, transcendentals=0),
        name=name,
    )


IN_VMEM = pl.BlockSpec(memory_space=pltpu.VMEM)
IN_SMEM = pl.BlockSpec(memory_space=pltpu.SMEM)
ANYWHERE = pl.BlockSpec(memory_space=pl.ANY)


def block_in_slot(assign_ref, slot):
    found = jnp.int32(0)
    for block in range(assign_ref.shape[1]):
        found = jnp.where(assign_ref[0, block] == slot, jnp.int32(block), found)
    return found


def tile_at(index, width):
    return pl.ds(pl.multiple_of(index * width, width), width)


def fold(tile):
    half = tile.shape[0] // 2
    row = lax.broadcasted_iota(jnp.int32, (half, 2 * half), 0)
    lane = lax.broadcasted_iota(jnp.int32, (half, 2 * half), 1)
    top, bottom = tile[:half, :], tile[half:, :]
    folded = jnp.where((lane < half) & (row > lane), pltpu.roll(bottom, half, 1), top)
    diagonal = jnp.sum(jnp.where(lane - half == row, bottom, 0.0), axis=0, keepdims=True)
    return folded, diagonal


def unfold(folded, diagonal):
    half = folded.shape[0]
    row = lax.broadcasted_iota(jnp.int32, (half, 2 * half), 0)
    lane = lax.broadcasted_iota(jnp.int32, (half, 2 * half), 1)
    turned = jnp.concatenate([folded, jnp.zeros_like(folded)], axis=0).T
    top = jnp.where((lane < half) & (row > lane), turned[:half, :], folded)
    last = jnp.where(
        lane - half < row,
        pltpu.roll(folded, half, 1),
        jnp.where(lane - half > row, pltpu.roll(turned[:half, :], half, 1), diagonal),
    )
    return jnp.concatenate([top, jnp.where(lane < half, turned[half:, :], last)], axis=0)


def pack_stats_kernel(
    slots, me_ref, assign_hbm, stats_hbm, near_ref, far2_ref, far3_ref, assign_ref, stats_ref, sems
):
    table = pltpu.make_async_copy(assign_hbm, assign_ref, sems.at[0])
    table.start()
    blocks = pltpu.make_async_copy(stats_hbm, stats_ref, sems.at[1])
    blocks.start()
    me = me_ref[0]
    width = stats_ref.shape[2]
    half = width // 2
    odd = me % 2
    table.wait()
    blocks.wait()
    for slot in range(slots):
        for far, out in ((2, far2_ref), (3, far3_ref)):
            block = block_in_slot(assign_ref, (me ^ far) * slots + slot)
            between = stats_ref[0, block, :, tile_at(me ^ 1, width)].astype(F32)
            out[slot, :half, :] = jnp.where(odd == 1, between.T[half:, :], between[:half, :]).astype(
                BF16
            )
            folded, diagonal = fold(stats_ref[0, block, :, tile_at(me, width)].astype(F32))
            out[slot, half:width, :] = folded.astype(BF16)
            out[slot, width:, :] = jnp.broadcast_to(diagonal, (DIAGONAL_ROWS, width)).astype(BF16)
    for slot in range(slots):
        block = block_in_slot(assign_ref, (me ^ 1) * slots + slot)
        for place, other in enumerate((0, 2, 3)):
            near_ref[slot, :, place * width : (place + 1) * width] = stats_ref[
                0, block, :, tile_at(me ^ other, width)
            ]


def pack_stats(me, assign, stats, slots):
    width, order = stats.shape[2:]
    near = jax.ShapeDtypeStruct((slots, width, order - width), BF16)
    far = jax.ShapeDtypeStruct((slots, width + DIAGONAL_ROWS, width), BF16)
    return call(
        functools.partial(pack_stats_kernel, slots),
        (near, far, far),
        [IN_SMEM, ANYWHERE, ANYWHERE],
        (IN_VMEM,) * 3,
        "pack_stats",
        scratch=[
            pltpu.SMEM(assign.shape, jnp.int32),
            pltpu.VMEM(stats.shape, BF16),
            pltpu.SemaphoreType.DMA((2,)),
        ],
        moved=2 * stats.size * 2,
    )(me, assign, stats)


def pack_grad_kernel(slots, me_ref, assign_ref, grad_ref, *outs):
    me = me_ref[0]
    for far in (3, 2, 1):
        for slot in range(slots):
            block = block_in_slot(assign_ref, (me ^ far) * slots + slot)
            outs[far - 1][slot] = grad_ref[0, block]


def pack_grad(me, assign, grad, slots):
    out = jax.ShapeDtypeStruct((slots, *grad.shape[2:]), BF16)
    return call(
        functools.partial(pack_grad_kernel, slots),
        (out,) * 3,
        [IN_SMEM, IN_SMEM, IN_VMEM],
        (IN_VMEM,) * 3,
        "pack_grad",
        moved=2 * grad.size * 2,
    )(me, assign, grad)


def root_kernel(
    slots,
    me_ref,
    assign_ref,
    due_ref,
    cost_ref,
    stats_ref,
    near_ref,
    far2_ref,
    far3_ref,
    stale_ref,
    root_ref,
    factor_ref,
    own,
    full,
    half_root,
    correction,
    sem,
    stale_sem,
):
    me = me_ref[0]
    order = full.shape[0]
    width = near_ref.shape[1]
    half = width // 2
    chunk = order // 2
    rows = [pl.ds(start, chunk) for start in range(0, order, chunk)]

    def eye_rows(start):
        r = lax.broadcasted_iota(jnp.int32, (chunk, order), 0) + start
        c = lax.broadcasted_iota(jnp.int32, (chunk, order), 1)
        return jnp.where(r == c, F32(1.5), F32(0.0))

    def assemble(slot, block):
        copy = pltpu.make_async_copy(stats_ref.at[0, block], own, sem)
        copy.start()
        even, odd = (me ^ 2) & 2, ((me ^ 2) & 2) + 1
        at = lambda index: tile_at(index, width)
        two, three = me ^ 2, me ^ 3
        for index, far_ref in ((two, far2_ref), (three, far3_ref)):
            full[at(index), at(index)] = unfold(
                far_ref[slot, half:width, :].astype(F32),
                far_ref[slot, width : width + 1, :].astype(F32),
            )
        from_two = far2_ref[slot, :half, :].astype(F32)
        from_three = far3_ref[slot, :half, :].astype(F32)
        two_is_even = me % 2 == 0
        between = jnp.concatenate(
            [
                jnp.where(two_is_even, from_two, from_three),
                jnp.where(two_is_even, from_three, from_two),
            ],
            axis=0,
        )
        full[at(even), at(odd)] = between
        full[at(odd), at(even)] = between.T
        near = me ^ 1
        for place, other in enumerate((0, 2, 3)):
            tile = near_ref[slot, :, place * width : (place + 1) * width].astype(F32)
            full[at(near), at(near ^ other)] = tile
            if other:
                full[at(near ^ other), at(near)] = tile.T
        copy.wait()
        full[at(me), :] = own[...].astype(F32)
        for other in (1, 2, 3):
            full[at(me ^ other), at(me)] = own[:, at(me ^ other)].astype(F32).T

    for slot in range(slots):
        block = block_in_slot(assign_ref, me * slots + slot)
        due = due_ref[0, block]
        cost = cost_ref[0, block]
        factor_ref[slot] = F32(1.0)

        @pl.when(due <= 0)
        def _():
            copy = pltpu.make_async_copy(stale_ref.at[0, slot], root_ref.at[slot], stale_sem)
            copy.start()
            copy.wait()

        @pl.when(due > 0)
        def _():
            assemble(slot, block)
            total = jnp.zeros((8, order), F32)
            for start in range(0, order, 8):
                piece = full[start : start + 8, :]
                total = total + piece * piece
            norm = jnp.sqrt(jnp.full((8, 128), jnp.sum(total), F32))
            factor_ref[slot] = lax.rsqrt(norm)[0, 0]
            divisor = jnp.max(norm)
            for i, start in enumerate(range(0, order, chunk)):
                scaled = (full[rows[i], :] / divisor).astype(BF16)
                half_root[rows[i], :] = scaled
                root_ref[slot, rows[i], :] = (eye_rows(start) - 0.5 * scaled.astype(F32)).astype(
                    BF16
                )

            @pl.when(cost > 1)
            def _():
                first = [
                    jnp.dot(half_root[r, :], root_ref[slot], preferred_element_type=F32).astype(BF16)
                    for r in rows
                ]
                for r, value in zip(rows, first):
                    half_root[r, :] = value

                def correct():
                    for i, start in enumerate(range(0, order, chunk)):
                        product = jnp.dot(
                            root_ref[slot, rows[i], :], half_root[...], preferred_element_type=F32
                        )
                        correction[rows[i], :] = (eye_rows(start) - 0.5 * product).astype(BF16)

                def next_root():
                    values = [
                        jnp.dot(
                            correction[r, :], root_ref[slot], preferred_element_type=F32
                        ).astype(BF16)
                        for r in rows
                    ]
                    for r, value in zip(rows, values):
                        root_ref[slot, r, :] = value

                def sweep(step, carry):
                    correct()
                    values = [
                        jnp.dot(
                            half_root[r, :], correction[...], preferred_element_type=F32
                        ).astype(BF16)
                        for r in rows
                    ]
                    for r, value in zip(rows, values):
                        half_root[r, :] = value
                    next_root()
                    return carry

                lax.fori_loop(0, cost - 2, sweep, 0)
                correct()
                next_root()


def roots(me, assign, due, cost, stats, received, stale, slots):
    order = stats.shape[3]
    width = stats.shape[2]
    return call(
        functools.partial(root_kernel, slots),
        (
            jax.ShapeDtypeStruct((slots, order, order), BF16),
            jax.ShapeDtypeStruct((slots,), F32),
        ),
        [IN_SMEM] * 4 + [ANYWHERE] + [IN_VMEM] * 3 + [ANYWHERE],
        (IN_VMEM, IN_SMEM),
        "roots",
        scratch=[
            pltpu.VMEM((width, order), BF16),
            pltpu.VMEM((order, order), F32),
            pltpu.VMEM((order, order), BF16),
            pltpu.VMEM((order, order), BF16),
            pltpu.SemaphoreType.DMA,
            pltpu.SemaphoreType.DMA,
        ],
        flops=slots * 9 * 2 * order**3,
        moved=slots * order * order * 6,
    )(me, assign, due, cost, stats, *received, stale)


def pair_product(slots, pair, odd, root_ref, factor_ref, whole_ref, first_ref, second_ref, sum_ref):
    rows, columns = first_ref.shape[1:]
    at = tile_at(pair, 2 * rows)
    total = jnp.zeros(sum_ref.shape, F32)
    for slot in range(slots):
        piece = jnp.dot(root_ref[slot, at, :], whole_ref[slot], preferred_element_type=F32)
        rounded = (piece * factor_ref[slot]).astype(BF16)
        low, high = rounded[:rows, :], rounded[rows:, :]
        first_ref[slot] = jnp.where(odd, high, low)
        second_ref[slot] = jnp.where(odd, low, high)
        terms = rounded.astype(F32) * whole_ref[slot, at, :].astype(F32)
        for start in range(0, 2 * rows, 8):
            for column in range(0, columns, 128):
                total = total + terms[start : start + 8, column : column + 128]
    sum_ref[...] = total


def far_kernel(
    slots,
    me_ref,
    assign_ref,
    root_ref,
    factor_ref,
    grad_ref,
    near_ref,
    far2_ref,
    far3_ref,
    out2_ref,
    out3_ref,
    sum_ref,
    whole_ref,
):
    me = me_ref[0]
    rows = near_ref.shape[1]
    for slot in range(slots):
        block = block_in_slot(assign_ref, me * slots + slot)
        whole_ref[slot, tile_at(me, rows), :] = grad_ref[0, block]
        for far, piece_ref in ((1, near_ref), (2, far2_ref), (3, far3_ref)):
            whole_ref[slot, tile_at(me ^ far, rows), :] = piece_ref[slot]
    pair_product(
        slots, 1 - me // 2, me % 2 == 1, root_ref, factor_ref, whole_ref, out2_ref, out3_ref, sum_ref
    )


def near_kernel(
    slots, me_ref, root_ref, factor_ref, whole_ref, far_sum_ref, own_ref, out1_ref, sum_ref
):
    me = me_ref[0]
    pair_product(
        slots, me // 2, me % 2 == 1, root_ref, factor_ref, whole_ref, own_ref, out1_ref, sum_ref
    )
    sum_ref[...] += far_sum_ref[...]


def products(slots, me, assign, root, factor, grad, pieces):
    rows, columns = pieces[0].shape[1:]
    order = root.shape[1]
    half = jax.ShapeDtypeStruct((slots, rows, columns), BF16)
    part = jax.ShapeDtypeStruct((8, 128), F32)
    cost = dict(
        flops=slots * order * order * columns, moved=slots * (order + columns) * order * 2
    )
    out2, out3, far_sum, whole = call(
        functools.partial(far_kernel, slots),
        (half, half, part, jax.ShapeDtypeStruct((slots, order, columns), BF16)),
        [IN_SMEM, IN_SMEM, IN_VMEM, IN_SMEM] + [IN_VMEM] * 4,
        (IN_VMEM,) * 4,
        "far_product",
        **cost,
    )(me, assign, root, factor, grad, *pieces)
    own, out1, total = call(
        functools.partial(near_kernel, slots),
        (half, half, part),
        [IN_SMEM, IN_VMEM, IN_SMEM, IN_VMEM, IN_VMEM],
        (IN_VMEM,) * 3,
        "near_product",
        **cost,
    )(me, root, factor, whole, far_sum)
    return (own, out1, out2, out3), total


def clip_kernel(slots, elements, me_ref, assign_ref, *rest):
    sums, rows, out_hbm, out_ref, sems = rest[:4], rest[4:8], *rest[8:]
    me = me_ref[0]
    quadratic = jnp.sum(sums[0][...] + sums[1][...] + sums[2][...] + sums[3][...])
    ratio = jnp.full((8, 128), F32(KL_BOUND * elements)) / quadratic
    clip_factor = jnp.max(jnp.minimum(F32(1.0), jnp.sqrt(ratio)))
    copies = []
    for far in range(4):
        for slot in range(slots):
            at = far * slots + slot
            block = block_in_slot(assign_ref, (me ^ far) * slots + slot)
            out_ref[at] = (clip_factor * rows[far][slot].astype(F32)).astype(BF16)
            copies.append(pltpu.make_async_copy(out_ref.at[at], out_hbm.at[0, block], sems.at[at]))
            copies[-1].start()
    for copy in copies:
        copy.wait()


def clip(me, assign, sums, rows, shape, slots, elements):
    return call(
        functools.partial(clip_kernel, slots, elements),
        jax.ShapeDtypeStruct(shape, BF16),
        [IN_SMEM, IN_SMEM] + [IN_VMEM] * (len(sums) + len(rows)),
        ANYWHERE,
        "clip",
        scratch=[pltpu.VMEM(shape[1:], BF16), pltpu.SemaphoreType.DMA((shape[1],))],
        moved=4 * shape[1] * shape[2] * shape[3],
    )(me, assign, *sums, *rows)


def after_kernel(value_ref, landed_ref, out_ref):
    out_ref[...] = value_ref[...]


def after(value, landed):
    return call(
        after_kernel,
        jax.ShapeDtypeStruct(value.shape, value.dtype),
        [IN_VMEM, ANYWHERE],
        IN_VMEM,
        "after",
    )(value, landed)


def partner_of(value, axis, far):
    count = lax.axis_size(axis)
    return lax.ppermute(value, axis, [(i, i ^ far) for i in range(count)])


def sum_over(value, axis):
    count = lax.axis_size(axis)
    total = value
    for shift in range(1, count):
        total = total + lax.ppermute(
            value, axis, [(i, (i + shift) % count) for i in range(count)]
        )
    return total


def exchange_four(stats, grad, due, cost, assign, stale):
    me = lax.axis_index("fsdp").astype(jnp.int32).reshape(1)
    slots = assign.shape[1] // 4
    near, far2, far3 = pack_stats(me, assign, stats, slots)
    received = [partner_of(near, "fsdp", 1), partner_of(far2, "fsdp", 2), partner_of(far3, "fsdp", 3)]
    sent = pack_grad(me, assign, grad, slots)
    pieces = [partner_of(piece, "fsdp", far) for far, piece in enumerate(sent, 1)]
    root, factor = roots(me, assign, due, cost, stats, received, stale, slots)
    solved, total = products(slots, me, assign, root, factor, grad, pieces)
    rows = [solved[0]] + [partner_of(solved[far], "fsdp", far) for far in (1, 2, 3)]
    total = sum_over(total, "dp")
    sums = [total, partner_of(after(total, rows[1]), "fsdp", 1)]
    sums += [partner_of(total, "fsdp", far) for far in (2, 3)]
    elements = lax.axis_size("dp") * assign.shape[1] * stats.shape[3] * grad.shape[3]
    return clip(me, assign, sums, rows, grad.shape, slots, elements)


def solution(mesh):
    return jax.shard_map(
        exchange_four if mesh.shape["fsdp"] == 4 else exchange_all,
        mesh=mesh,
        in_specs=(
            P(("groups", "dp"), None, "fsdp", None),
            P(("groups", "dp"), None, "fsdp", None),
            P(("groups", "dp"), None),
            P(("groups", "dp"), None),
            P(("groups", "dp"), None),
            P(("groups", "dp"), "fsdp", None, None),
        ),
        out_specs=P(("groups", "dp"), None, "fsdp", None),
        check_vma=False,
    )
```

```python
import functools

import jax
import jax.numpy as jnp
from jax import lax
from jax.experimental import pallas as pl
from jax.experimental.pallas import tpu as pltpu
from jax.sharding import PartitionSpec as P

KL_BOUND = 1.0
VMEM_BYTES = 40 * 2**20
DIAGONAL_ROWS = 16
F32 = jnp.float32
BF16 = jnp.bfloat16


def refresh(block_piece, grad_rows, old_root, due_flag, sweep_count):
    full_block = block_piece.astype(F32)
    frobenius = jnp.sqrt(jnp.sum(full_block * full_block))
    identity = jnp.eye(full_block.shape[0], dtype=F32)
    root_half = (full_block / frobenius).astype(BF16)
    root_inverse = identity.astype(BF16)

    def sweep(step_index, iterates):
        half_now, inverse_now = iterates
        product = jnp.dot(inverse_now, half_now, preferred_element_type=F32)
        correction = (1.5 * identity - 0.5 * product).astype(BF16)
        half_next = jnp.dot(half_now, correction, preferred_element_type=F32).astype(BF16)
        inverse_next = jnp.dot(correction, inverse_now, preferred_element_type=F32).astype(BF16)
        return (half_next, inverse_next)

    root_half, root_inverse = lax.fori_loop(0, sweep_count, sweep, (root_half, root_inverse))
    left_factor = jnp.where(due_flag > 0, root_inverse, old_root)
    factor = jnp.where(due_flag > 0, lax.rsqrt(frobenius), F32(1.0))
    return (jnp.dot(left_factor, grad_rows, preferred_element_type=F32) * factor).astype(BF16)


def exchange_all(stats, grad, due, cost, assign, stale):
    own_index = lax.axis_index("fsdp")
    solver_count = lax.axis_size("fsdp")
    dp_count = lax.axis_size("dp")
    table_row = assign[0]
    due_row = due[0]
    cost_row = cost[0]
    total_slots = table_row.shape[0]
    slot_count = total_slots // solver_count
    row_count = stats.shape[2]
    block_order = stats.shape[3]
    column_count = grad.shape[3]
    source = jnp.argsort(table_row, stable=True)
    sent_stats = jnp.take(stats[0], source, axis=0).reshape(
        solver_count, slot_count, row_count, block_order
    )
    sent_grad = jnp.take(grad[0], source, axis=0).reshape(
        solver_count, slot_count, row_count, column_count
    )
    blocks_here, grads_here = (
        lax.all_to_all(sent_stats, "fsdp", split_axis=0, concat_axis=2, tiled=True),
        lax.all_to_all(sent_grad, "fsdp", split_axis=0, concat_axis=2, tiled=True),
    )
    my_blocks = lax.dynamic_slice_in_dim(source, own_index * slot_count, slot_count)
    results = []
    for slot in range(slot_count):
        block_id = my_blocks[slot]
        due_flag = due_row[block_id]
        results.append(
            refresh(
                blocks_here[0, slot],
                grads_here[0, slot],
                stale[0, slot],
                due_flag,
                cost_row[block_id] * due_flag,
            )
        )
    solved = jnp.stack(results)
    returned = lax.all_to_all(
        solved.reshape(slot_count, solver_count, row_count, column_count),
        "fsdp",
        split_axis=1,
        concat_axis=0,
        tiled=True,
    )
    owner_rows = jnp.take(returned.reshape(total_slots, row_count, column_count), table_row, axis=0)
    local_part = jnp.sum(owner_rows.astype(F32) * grad[0].astype(F32))
    quadratic = lax.psum(local_part, ("fsdp", "dp"))
    elements = dp_count * total_slots * block_order * column_count
    clip_factor = jnp.minimum(F32(1.0), jnp.sqrt(KL_BOUND * elements / quadratic))
    return (clip_factor * owner_rows.astype(F32)).astype(BF16)[None]


def call(kernel, out_shape, in_specs, out_specs, name, scratch=(), flops=0, moved=0):
    return pl.pallas_call(
        kernel,
        out_shape=out_shape,
        in_specs=in_specs,
        out_specs=out_specs,
        scratch_shapes=list(scratch),
        compiler_params=pltpu.CompilerParams(vmem_limit_bytes=VMEM_BYTES),
        cost_estimate=pl.CostEstimate(flops=flops, bytes_accessed=moved, transcendentals=0),
        name=name,
    )


IN_VMEM = pl.BlockSpec(memory_space=pltpu.VMEM)
IN_SMEM = pl.BlockSpec(memory_space=pltpu.SMEM)
ANYWHERE = pl.BlockSpec(memory_space=pl.ANY)


def plan_of(table_row):
    total = table_row.shape[0]
    blocks = lax.broadcasted_iota(jnp.int32, (total + 1, total), 1)
    slots = lax.broadcasted_iota(jnp.int32, (total + 1, total), 0)
    source = jnp.sum(jnp.where(table_row[None, :] == slots, blocks, 0), axis=1)
    place = lax.axis_index("fsdp").astype(jnp.int32)
    return jnp.where(jnp.arange(total + 1) == total, place, source)


def place_of(plan_ref):
    return plan_ref[plan_ref.shape[0] - 1]


def tile_at(index, width):
    return pl.ds(pl.multiple_of(index * width, width), width)


def fold(tile):
    half = tile.shape[0] // 2
    row = lax.broadcasted_iota(jnp.int32, (half, 2 * half), 0)
    lane = lax.broadcasted_iota(jnp.int32, (half, 2 * half), 1)
    top, bottom = tile[:half, :], tile[half:, :]
    folded = jnp.where((lane < half) & (row > lane), pltpu.roll(bottom, half, 1), top)
    diagonal = jnp.sum(jnp.where(lane - half == row, bottom, 0.0), axis=0, keepdims=True)
    return folded, diagonal


def unfold(folded, diagonal):
    half = folded.shape[0]
    row = lax.broadcasted_iota(jnp.int32, (half, 2 * half), 0)
    lane = lax.broadcasted_iota(jnp.int32, (half, 2 * half), 1)
    turned = jnp.concatenate([folded, jnp.zeros_like(folded)], axis=0).T
    top = jnp.where((lane < half) & (row > lane), turned[:half, :], folded)
    last = jnp.where(
        lane - half < row,
        pltpu.roll(folded, half, 1),
        jnp.where(lane - half > row, pltpu.roll(turned[:half, :], half, 1), diagonal),
    )
    return jnp.concatenate([top, jnp.where(lane < half, turned[half:, :], last)], axis=0)


def pack_stats_kernel(slots, plan_ref, stats_ref, near_ref, far2_ref, far3_ref):
    me = place_of(plan_ref)
    width = stats_ref.shape[2]
    half = width // 2
    odd = me % 2
    for far, out in ((2, far2_ref), (3, far3_ref)):
        diagonals = []
        for slot in range(slots):
            block = plan_ref[(me ^ far) * slots + slot]
            between = stats_ref[0, block, :, tile_at(me ^ 1, width)].astype(F32)
            at = slot * width
            out[at : at + half, :] = jnp.where(
                odd == 1, between.T[half:, :], between[:half, :]
            ).astype(BF16)
            folded, diagonal = fold(stats_ref[0, block, :, tile_at(me, width)].astype(F32))
            out[at + half : at + width, :] = folded.astype(BF16)
            diagonals.append(diagonal)
        lane = lax.broadcasted_iota(jnp.int32, (1, width), 1)
        for start in range(0, slots, 2):
            pair = pltpu.roll(diagonals[start], half, 1)
            if start + 1 < slots:
                pair = jnp.where(lane < half, pair, diagonals[start + 1])
            at = slots * width + start // 2 * DIAGONAL_ROWS
            out[at : at + DIAGONAL_ROWS, :] = jnp.broadcast_to(pair, (DIAGONAL_ROWS, width)).astype(
                BF16
            )
    for slot in range(slots):
        block = plan_ref[(me ^ 1) * slots + slot]
        for place, other in enumerate((0, 2, 3)):
            near_ref[slot, :, place * width : (place + 1) * width] = stats_ref[
                0, block, :, tile_at(me ^ other, width)
            ]


def pack_stats(plan, stats, slots):
    width, order = stats.shape[2:]
    near = jax.ShapeDtypeStruct((slots, width, order - width), BF16)
    far = jax.ShapeDtypeStruct((slots * width + (slots + 1) // 2 * DIAGONAL_ROWS, width), BF16)
    return call(
        functools.partial(pack_stats_kernel, slots),
        (near, far, far),
        [IN_SMEM, IN_VMEM],
        (IN_VMEM,) * 3,
        "pack_stats",
        moved=2 * stats.size * 2,
    )(plan, stats)


def pack_grad_kernel(slots, plan_ref, grad_ref, *outs):
    me = place_of(plan_ref)
    for far in (3, 2, 1, 0):
        for slot in range(slots):
            outs[far][slot] = grad_ref[0, plan_ref[(me ^ far) * slots + slot]]


def pack_grad(plan, grad, slots):
    out = jax.ShapeDtypeStruct((slots, *grad.shape[2:]), BF16)
    return call(
        functools.partial(pack_grad_kernel, slots),
        (out,) * 4,
        [IN_SMEM, IN_VMEM],
        (IN_VMEM,) * 4,
        "pack_grad",
        moved=2 * grad.size * 2,
    )(plan, grad)


def root_kernel(
    slots,
    plan_ref,
    due_ref,
    cost_ref,
    stats_ref,
    near_ref,
    far2_ref,
    far3_ref,
    stale_ref,
    root_ref,
    factor_ref,
    own,
    full,
    half_root,
    correction,
    sem,
    stale_sem,
):
    me = place_of(plan_ref)
    order = full.shape[0]
    width = near_ref.shape[1]
    half = width // 2
    chunk = order // 2
    rows = [pl.ds(start, chunk) for start in range(0, order, chunk)]

    def eye_rows(start):
        r = lax.broadcasted_iota(jnp.int32, (chunk, order), 0) + start
        c = lax.broadcasted_iota(jnp.int32, (chunk, order), 1)
        return jnp.where(r == c, F32(1.5), F32(0.0))

    def assemble(slot, block):
        copy = pltpu.make_async_copy(stats_ref.at[0, block], own, sem)
        copy.start()
        even, odd = (me ^ 2) & 2, ((me ^ 2) & 2) + 1
        at = lambda index: tile_at(index, width)
        two, three = me ^ 2, me ^ 3
        start = slot * width
        row = slots * width + slot // 2 * DIAGONAL_ROWS
        for index, far_ref in ((two, far2_ref), (three, far3_ref)):
            diagonal = far_ref[row : row + 8, :].astype(F32)
            if slot % 2 == 0:
                diagonal = pltpu.roll(diagonal, half, 1)
            full[at(index), at(index)] = unfold(
                far_ref[start + half : start + width, :].astype(F32), diagonal[:1, :]
            )
        from_two = far2_ref[start : start + half, :].astype(F32)
        from_three = far3_ref[start : start + half, :].astype(F32)
        two_is_even = me % 2 == 0
        between = jnp.concatenate(
            [
                jnp.where(two_is_even, from_two, from_three),
                jnp.where(two_is_even, from_three, from_two),
            ],
            axis=0,
        )
        full[at(even), at(odd)] = between
        full[at(odd), at(even)] = between.T
        near = me ^ 1
        for place, other in enumerate((0, 2, 3)):
            tile = near_ref[slot, :, place * width : (place + 1) * width].astype(F32)
            full[at(near), at(near ^ other)] = tile
            if other:
                full[at(near ^ other), at(near)] = tile.T
        copy.wait()
        full[at(me), :] = own[...].astype(F32)
        for other in (1, 2, 3):
            full[at(me ^ other), at(me)] = own[:, at(me ^ other)].astype(F32).T

    for slot in range(slots):
        block = plan_ref[me * slots + slot]
        due = due_ref[0, block]
        cost = cost_ref[0, block]
        factor_ref[slot] = jnp.ones((8, 128), F32)

        @pl.when(due <= 0)
        def _():
            copy = pltpu.make_async_copy(stale_ref.at[0, slot], root_ref.at[slot], stale_sem)
            copy.start()
            copy.wait()

        @pl.when(due > 0)
        def _():
            assemble(slot, block)
            total = jnp.zeros((8, order), F32)
            for start in range(0, order, 8):
                piece = full[start : start + 8, :]
                total = total + piece * piece
            norm = jnp.sqrt(jnp.full((8, 128), jnp.sum(total), F32))
            factor_ref[slot] = lax.rsqrt(norm)
            divisor = jnp.max(norm)
            for i, start in enumerate(range(0, order, chunk)):
                scaled = (full[rows[i], :] / divisor).astype(BF16)
                half_root[rows[i], :] = scaled
                root_ref[slot, rows[i], :] = (eye_rows(start) - 0.5 * scaled.astype(F32)).astype(
                    BF16
                )

            @pl.when(cost > 1)
            def _():
                first = [
                    jnp.dot(half_root[r, :], root_ref[slot], preferred_element_type=F32).astype(BF16)
                    for r in rows
                ]
                for r, value in zip(rows, first):
                    half_root[r, :] = value

                def correct():
                    for i, start in enumerate(range(0, order, chunk)):
                        product = jnp.dot(
                            root_ref[slot, rows[i], :], half_root[...], preferred_element_type=F32
                        )
                        correction[rows[i], :] = (eye_rows(start) - 0.5 * product).astype(BF16)

                def next_root():
                    values = [
                        jnp.dot(
                            correction[r, :], root_ref[slot], preferred_element_type=F32
                        ).astype(BF16)
                        for r in rows
                    ]
                    for r, value in zip(rows, values):
                        root_ref[slot, r, :] = value

                def sweep(step, carry):
                    correct()
                    values = [
                        jnp.dot(
                            half_root[r, :], correction[...], preferred_element_type=F32
                        ).astype(BF16)
                        for r in rows
                    ]
                    for r, value in zip(rows, values):
                        half_root[r, :] = value
                    next_root()
                    return carry

                lax.fori_loop(0, cost - 2, sweep, 0)
                correct()
                next_root()


def roots(plan, due, cost, stats, received, stale, slots):
    order = stats.shape[3]
    width = stats.shape[2]
    return call(
        functools.partial(root_kernel, slots),
        (
            jax.ShapeDtypeStruct((slots, order, order), BF16),
            jax.ShapeDtypeStruct((slots, 8, 128), F32),
        ),
        [IN_SMEM] * 3 + [ANYWHERE] + [IN_VMEM] * 3 + [ANYWHERE],
        (IN_VMEM, IN_VMEM),
        "roots",
        scratch=[
            pltpu.VMEM((width, order), BF16),
            pltpu.VMEM((order, order), F32),
            pltpu.VMEM((order, order), BF16),
            pltpu.VMEM((order, order), BF16),
            pltpu.SemaphoreType.DMA,
            pltpu.SemaphoreType.DMA,
        ],
        flops=slots * 9 * 2 * order**3,
        moved=slots * order * order * 6,
    )(plan, due, cost, stats, *received, stale)


def start_kernel(
    slots,
    plan_ref,
    root_ref,
    own_ref,
    grad1_ref,
    far_root_ref,
    near_root_ref,
    far_ref,
    near_ref,
    columns_ref,
):
    me = place_of(plan_ref)
    width = grad1_ref.shape[1]
    for slot in range(slots):
        here = jnp.concatenate([own_ref[slot], grad1_ref[slot]], axis=0)
        for places, root_out, out in (((2, 3), far_root_ref, far_ref), ((0, 1), near_root_ref, near_ref)):
            for i, row in enumerate(places):
                rows = tile_at(me ^ row, width)
                for j in range(2):
                    at = (slice(i * width, (i + 1) * width), slice(j * width, (j + 1) * width))
                    root_out[slot, at[0], at[1]] = root_ref[slot, rows, tile_at(me ^ (2 + j), width)]
                    columns_ref[at[0], at[1]] = root_ref[slot, rows, tile_at(me ^ j, width)]
            out[slot] = jnp.dot(columns_ref[...], here, preferred_element_type=F32)


def start_product(plan, root, own_grad, grad1):
    slots, width, columns = grad1.shape
    pair = jax.ShapeDtypeStruct((slots, 2 * width, 2 * width), BF16)
    total = jax.ShapeDtypeStruct((slots, 2 * width, columns), F32)
    return call(
        functools.partial(start_kernel, slots),
        (pair, pair, total, total),
        [IN_SMEM] + [IN_VMEM] * 3,
        (IN_VMEM,) * 4,
        "start_product",
        scratch=[pltpu.VMEM((2 * width, 2 * width), BF16)],
        flops=slots * 16 * width * width * columns,
        moved=slots * 16 * width * columns,
    )(plan, root, own_grad, grad1)


def finish_kernel(root_ref, begun_ref, factor_ref, grad2_ref, grad3_ref, *rest):
    first_ref, second_ref = rest[-2:] if len(rest) == 2 else rest[-3:-1]
    slots, width, columns = first_ref.shape
    total = jnp.zeros((8, 128), F32)
    for slot in range(slots):
        there = jnp.concatenate([grad2_ref[slot], grad3_ref[slot]], axis=0)
        product = begun_ref[slot] + jnp.dot(root_ref[slot], there, preferred_element_type=F32)
        rounded = (product * factor_ref[slot, :1, :1]).astype(BF16)
        first_ref[slot] = rounded[:width, :]
        second_ref[slot] = rounded[width:, :]
    if len(rest) > 2:
        own_ref, grad1_ref, out2_ref, out3_ref = rest[:4]
        for slot in range(slots):
            for result_ref, with_ref in (
                (first_ref, own_ref),
                (second_ref, grad1_ref),
                (out2_ref, grad2_ref),
                (out3_ref, grad3_ref),
            ):
                terms = result_ref[slot].astype(F32) * with_ref[slot].astype(F32)
                for start in range(0, width, 8):
                    for column in range(0, columns, 128):
                        total = total + terms[start : start + 8, column : column + 128]
        rest[-1][...] = total


def finish_product(root, begun, factor, grad2, grad3, *others):
    slots, width, columns = grad2.shape
    out = jax.ShapeDtypeStruct(grad2.shape, BF16)
    shapes = (out, out) + ((jax.ShapeDtypeStruct((8, 128), F32),) if others else ())
    return call(
        finish_kernel,
        shapes,
        [IN_VMEM] * (5 + len(others)),
        (IN_VMEM,) * len(shapes),
        "near_product" if others else "far_product",
        flops=slots * 8 * width * width * columns,
        moved=slots * 16 * width * columns,
    )(root, begun, factor, grad2, grad3, *others)


def clip_kernel(slots, elements, plan_ref, *rest):
    sums, rows, out_hbm, out_ref, sems = rest[:4], rest[4:8], *rest[8:]
    me = place_of(plan_ref)
    quadratic = jnp.sum(sums[0][...] + sums[1][...] + sums[2][...] + sums[3][...])
    ratio = jnp.full((8, 128), F32(KL_BOUND * elements)) / quadratic
    clip_factor = jnp.max(jnp.minimum(F32(1.0), jnp.sqrt(ratio)))
    copies = []
    for far in range(4):
        for slot in range(slots):
            at = far * slots + slot
            block = plan_ref[(me ^ far) * slots + slot]
            out_ref[at] = (clip_factor * rows[far][slot].astype(F32)).astype(BF16)
            copies.append(pltpu.make_async_copy(out_ref.at[at], out_hbm.at[0, block], sems.at[at]))
            copies[-1].start()
    for copy in copies:
        copy.wait()


def clip(plan, sums, rows, shape, slots, elements):
    return call(
        functools.partial(clip_kernel, slots, elements),
        jax.ShapeDtypeStruct(shape, BF16),
        [IN_SMEM] + [IN_VMEM] * (len(sums) + len(rows)),
        ANYWHERE,
        "clip",
        scratch=[pltpu.VMEM(shape[1:], BF16), pltpu.SemaphoreType.DMA((shape[1],))],
        moved=4 * shape[1] * shape[2] * shape[3],
    )(plan, *sums, *rows)


def after_kernel(value_ref, landed_ref, out_ref):
    out_ref[...] = value_ref[...]


def after(value, landed):
    return call(
        after_kernel,
        jax.ShapeDtypeStruct(value.shape, value.dtype),
        [IN_VMEM, ANYWHERE],
        IN_VMEM,
        "after",
    )(value, landed)


def partner_of(value, axis, far):
    count = lax.axis_size(axis)
    return lax.ppermute(value, axis, [(i, i ^ far) for i in range(count)])


def sum_over(value, axis):
    count = lax.axis_size(axis)
    total = value
    for shift in range(1, count):
        total = total + lax.ppermute(
            value, axis, [(i, (i + shift) % count) for i in range(count)]
        )
    return total


def exchange_four(stats, grad, due, cost, assign, stale):
    slots = assign.shape[1] // 4
    plan = plan_of(assign[0])
    near, far2, far3 = pack_stats(plan, stats, slots)
    received = [partner_of(near, "fsdp", 1), partner_of(far2, "fsdp", 2), partner_of(far3, "fsdp", 3)]
    own_grad, *sent = pack_grad(plan, grad, slots)
    grad1, grad2, grad3 = [partner_of(piece, "fsdp", far) for far, piece in enumerate(sent, 1)]
    root, factor = roots(plan, due, cost, stats, received, stale, slots)
    far_root, near_root, far, near = start_product(plan, root, own_grad, grad1)
    out2, out3 = finish_product(far_root, far, factor, grad2, grad3)
    own, out1, total = finish_product(
        near_root, near, factor, grad2, grad3, own_grad, grad1, out2, out3
    )
    rows = [own] + [partner_of(out, "fsdp", far) for far, out in enumerate((out1, out2, out3), 1)]
    total = sum_over(total, "dp")
    sums = [total, partner_of(after(total, rows[2]), "fsdp", 1)]
    sums += [partner_of(total, "fsdp", far) for far in (2, 3)]
    elements = lax.axis_size("dp") * assign.shape[1] * stats.shape[3] * grad.shape[3]
    return clip(plan, sums, rows, grad.shape, slots, elements)


def solution(mesh):
    return jax.shard_map(
        exchange_four if mesh.shape["fsdp"] == 4 else exchange_all,
        mesh=mesh,
        in_specs=(
            P(("groups", "dp"), None, "fsdp", None),
            P(("groups", "dp"), None, "fsdp", None),
            P(("groups", "dp"), None),
            P(("groups", "dp"), None),
            P(("groups", "dp"), None),
            P(("groups", "dp"), "fsdp", None, None),
        ),
        out_specs=P(("groups", "dp"), None, "fsdp", None),
        check_vma=False,
    )
```

```python
import functools

import jax
import jax.numpy as jnp
from jax import lax
from jax.experimental import pallas as pl
from jax.experimental.pallas import tpu as pltpu
from jax.sharding import PartitionSpec as P

KL_BOUND = 1.0
VMEM_BYTES = 40 * 2**20
PACK_VMEM_BYTES = int(59 * 2**20)
DIAGONAL_ROWS = 16
F32 = jnp.float32
BF16 = jnp.bfloat16


def refresh(block_piece, grad_rows, old_root, due_flag, sweep_count):
    full_block = block_piece.astype(F32)
    frobenius = jnp.sqrt(jnp.sum(full_block * full_block))
    identity = jnp.eye(full_block.shape[0], dtype=F32)
    root_half = (full_block / frobenius).astype(BF16)
    root_inverse = identity.astype(BF16)

    def sweep(step_index, iterates):
        half_now, inverse_now = iterates
        product = jnp.dot(inverse_now, half_now, preferred_element_type=F32)
        correction = (1.5 * identity - 0.5 * product).astype(BF16)
        half_next = jnp.dot(half_now, correction, preferred_element_type=F32).astype(BF16)
        inverse_next = jnp.dot(correction, inverse_now, preferred_element_type=F32).astype(BF16)
        return (half_next, inverse_next)

    root_half, root_inverse = lax.fori_loop(0, sweep_count, sweep, (root_half, root_inverse))
    left_factor = jnp.where(due_flag > 0, root_inverse, old_root)
    factor = jnp.where(due_flag > 0, lax.rsqrt(frobenius), F32(1.0))
    return (jnp.dot(left_factor, grad_rows, preferred_element_type=F32) * factor).astype(BF16)


def exchange_all(stats, grad, due, cost, assign, stale):
    own_index = lax.axis_index("fsdp")
    solver_count = lax.axis_size("fsdp")
    dp_count = lax.axis_size("dp")
    table_row = assign[0]
    due_row = due[0]
    cost_row = cost[0]
    total_slots = table_row.shape[0]
    slot_count = total_slots // solver_count
    row_count = stats.shape[2]
    block_order = stats.shape[3]
    column_count = grad.shape[3]
    source = jnp.argsort(table_row, stable=True)
    sent_stats = jnp.take(stats[0], source, axis=0).reshape(
        solver_count, slot_count, row_count, block_order
    )
    sent_grad = jnp.take(grad[0], source, axis=0).reshape(
        solver_count, slot_count, row_count, column_count
    )
    blocks_here, grads_here = (
        lax.all_to_all(sent_stats, "fsdp", split_axis=0, concat_axis=2, tiled=True),
        lax.all_to_all(sent_grad, "fsdp", split_axis=0, concat_axis=2, tiled=True),
    )
    my_blocks = lax.dynamic_slice_in_dim(source, own_index * slot_count, slot_count)
    results = []
    for slot in range(slot_count):
        block_id = my_blocks[slot]
        due_flag = due_row[block_id]
        results.append(
            refresh(
                blocks_here[0, slot],
                grads_here[0, slot],
                stale[0, slot],
                due_flag,
                cost_row[block_id] * due_flag,
            )
        )
    solved = jnp.stack(results)
    returned = lax.all_to_all(
        solved.reshape(slot_count, solver_count, row_count, column_count),
        "fsdp",
        split_axis=1,
        concat_axis=0,
        tiled=True,
    )
    owner_rows = jnp.take(returned.reshape(total_slots, row_count, column_count), table_row, axis=0)
    local_part = jnp.sum(owner_rows.astype(F32) * grad[0].astype(F32))
    quadratic = lax.psum(local_part, ("fsdp", "dp"))
    elements = dp_count * total_slots * block_order * column_count
    clip_factor = jnp.minimum(F32(1.0), jnp.sqrt(KL_BOUND * elements / quadratic))
    return (clip_factor * owner_rows.astype(F32)).astype(BF16)[None]


def call(kernel, out_shape, in_specs, out_specs, name, scratch=(), flops=0, moved=0, vmem=VMEM_BYTES):
    return pl.pallas_call(
        kernel,
        out_shape=out_shape,
        in_specs=in_specs,
        out_specs=out_specs,
        scratch_shapes=list(scratch),
        compiler_params=pltpu.CompilerParams(vmem_limit_bytes=vmem),
        cost_estimate=pl.CostEstimate(flops=flops, bytes_accessed=moved, transcendentals=0),
        name=name,
    )


IN_VMEM = pl.BlockSpec(memory_space=pltpu.VMEM)
IN_SMEM = pl.BlockSpec(memory_space=pltpu.SMEM)
ANYWHERE = pl.BlockSpec(memory_space=pl.ANY)


def plan_of(table_row, place):
    total = table_row.shape[0]
    blocks = lax.broadcasted_iota(jnp.int32, (total + 1, total), 1)
    slots = lax.broadcasted_iota(jnp.int32, (total + 1, total), 0)
    source = jnp.sum(jnp.where(table_row[None, :] == slots, blocks, 0), axis=1)
    return jnp.where(jnp.arange(total + 1) == total, place, source)


def place_of(plan_ref):
    return plan_ref[plan_ref.shape[0] - 1]


def tile_at(index, width):
    return pl.ds(pl.multiple_of(index * width, width), width)


def fold(tile):
    half = tile.shape[0] // 2
    row = lax.broadcasted_iota(jnp.int32, (half, 2 * half), 0)
    lane = lax.broadcasted_iota(jnp.int32, (half, 2 * half), 1)
    top, bottom = tile[:half, :], tile[half:, :]
    folded = jnp.where((lane < half) & (row > lane), pltpu.roll(bottom, half, 1), top)
    diagonal = jnp.sum(jnp.where(lane - half == row, bottom, 0.0), axis=0, keepdims=True)
    return folded, diagonal


def unfold(folded, diagonal):
    half = folded.shape[0]
    row = lax.broadcasted_iota(jnp.int32, (half, 2 * half), 0)
    lane = lax.broadcasted_iota(jnp.int32, (half, 2 * half), 1)
    turned = jnp.concatenate([folded, jnp.zeros_like(folded)], axis=0).T
    top = jnp.where((lane < half) & (row > lane), turned[:half, :], folded)
    last = jnp.where(
        lane - half < row,
        pltpu.roll(folded, half, 1),
        jnp.where(lane - half > row, pltpu.roll(turned[:half, :], half, 1), diagonal),
    )
    return jnp.concatenate([top, jnp.where(lane < half, turned[half:, :], last)], axis=0)


def block_in_slot(assign_ref, slot):
    found = jnp.int32(0)
    for block in range(assign_ref.shape[1]):
        found = jnp.where(assign_ref[0, block] == slot, jnp.int32(block), found)
    return found


def pack_stats_kernel(
    slots, me_ref, assign_hbm, stats_hbm, near_ref, far2_ref, far3_ref, assign_ref, stats_ref, sems
):
    blocks = stats_ref.shape[1]
    table = pltpu.make_async_copy(assign_hbm, assign_ref, sems.at[blocks])
    table.start()
    copies = [
        pltpu.make_async_copy(stats_hbm.at[0, block], stats_ref.at[0, block], sems.at[block])
        for block in range(blocks)
    ]
    for copy in copies:
        copy.start()
    me = me_ref[0]
    width = stats_ref.shape[2]
    table.wait()
    for copy in copies:
        copy.wait()
    half = width // 2
    odd = me % 2
    for far, out in ((2, far2_ref), (3, far3_ref)):
        diagonals = []
        for slot in range(slots):
            block = block_in_slot(assign_ref, (me ^ far) * slots + slot)
            between = stats_ref[0, block, :, tile_at(me ^ 1, width)].astype(F32)
            at = slot * width
            out[at : at + half, :] = jnp.where(
                odd == 1, between.T[half:, :], between[:half, :]
            ).astype(BF16)
            folded, diagonal = fold(stats_ref[0, block, :, tile_at(me, width)].astype(F32))
            out[at + half : at + width, :] = folded.astype(BF16)
            diagonals.append(diagonal)
        lane = lax.broadcasted_iota(jnp.int32, (1, width), 1)
        for start in range(0, slots, 2):
            pair = pltpu.roll(diagonals[start], half, 1)
            if start + 1 < slots:
                pair = jnp.where(lane < half, pair, diagonals[start + 1])
            at = slots * width + start // 2 * DIAGONAL_ROWS
            out[at : at + DIAGONAL_ROWS, :] = jnp.broadcast_to(pair, (DIAGONAL_ROWS, width)).astype(
                BF16
            )
    for slot in range(slots):
        block = block_in_slot(assign_ref, (me ^ 1) * slots + slot)
        for place, other in enumerate((0, 2, 3)):
            near_ref[slot, :, place * width : (place + 1) * width] = stats_ref[
                0, block, :, tile_at(me ^ other, width)
            ]


def pack_stats(me, assign, stats, slots):
    width, order = stats.shape[2:]
    near = jax.ShapeDtypeStruct((slots, width, order - width), BF16)
    far = jax.ShapeDtypeStruct((slots * width + (slots + 1) // 2 * DIAGONAL_ROWS, width), BF16)
    return call(
        functools.partial(pack_stats_kernel, slots),
        (near, far, far),
        [IN_SMEM, ANYWHERE, ANYWHERE],
        (IN_VMEM,) * 3,
        "pack_stats",
        scratch=[
            pltpu.SMEM(assign.shape, jnp.int32),
            pltpu.VMEM(stats.shape, BF16),
            pltpu.SemaphoreType.DMA((stats.shape[1] + 1,)),
        ],
        moved=2 * stats.size * 2,
        vmem=PACK_VMEM_BYTES,
    )(me, assign, stats)


def pack_grad_kernel(slots, plan_ref, grad_ref, *outs):
    me = place_of(plan_ref)
    for far in (3, 2, 1, 0):
        for slot in range(slots):
            outs[far][slot] = grad_ref[0, plan_ref[(me ^ far) * slots + slot]]


def pack_grad(plan, grad, slots):
    out = jax.ShapeDtypeStruct((slots, *grad.shape[2:]), BF16)
    return call(
        functools.partial(pack_grad_kernel, slots),
        (out,) * 4,
        [IN_SMEM, IN_VMEM],
        (IN_VMEM,) * 4,
        "pack_grad",
        moved=2 * grad.size * 2,
    )(plan, grad)


def root_kernel(
    slots,
    plan_ref,
    due_ref,
    cost_ref,
    stats_ref,
    near_ref,
    far3_ref,
    far2_ref,
    stale_ref,
    root_ref,
    factor_ref,
    own,
    full,
    half_root,
    correction,
    sem,
    stale_sem,
):
    me = place_of(plan_ref)
    order = full.shape[0]
    width = near_ref.shape[1]
    half = width // 2
    chunk = order // 2
    rows = [pl.ds(start, chunk) for start in range(0, order, chunk)]

    def eye_rows(start):
        r = lax.broadcasted_iota(jnp.int32, (chunk, order), 0) + start
        c = lax.broadcasted_iota(jnp.int32, (chunk, order), 1)
        return jnp.where(r == c, F32(1.5), F32(0.0))

    def assemble(slot, block):
        copy = pltpu.make_async_copy(stats_ref.at[0, block], own, sem)
        copy.start()
        even, odd = (me ^ 2) & 2, ((me ^ 2) & 2) + 1
        at = lambda index: tile_at(index, width)
        two, three = me ^ 2, me ^ 3
        start = slot * width
        row = slots * width + slot // 2 * DIAGONAL_ROWS
        for index, far_ref in ((two, far2_ref), (three, far3_ref)):
            diagonal = far_ref[row : row + 8, :].astype(F32)
            if slot % 2 == 0:
                diagonal = pltpu.roll(diagonal, half, 1)
            full[at(index), at(index)] = unfold(
                far_ref[start + half : start + width, :].astype(F32), diagonal[:1, :]
            )
        from_two = far2_ref[start : start + half, :].astype(F32)
        from_three = far3_ref[start : start + half, :].astype(F32)
        two_is_even = me % 2 == 0
        between = jnp.concatenate(
            [
                jnp.where(two_is_even, from_two, from_three),
                jnp.where(two_is_even, from_three, from_two),
            ],
            axis=0,
        )
        full[at(even), at(odd)] = between
        full[at(odd), at(even)] = between.T
        near = me ^ 1
        for place, other in enumerate((0, 2, 3)):
            tile = near_ref[slot, :, place * width : (place + 1) * width].astype(F32)
            full[at(near), at(near ^ other)] = tile
            if other:
                full[at(near ^ other), at(near)] = tile.T
        copy.wait()
        full[at(me), :] = own[...].astype(F32)
        for other in (1, 2, 3):
            full[at(me ^ other), at(me)] = own[:, at(me ^ other)].astype(F32).T

    for slot in range(slots):
        block = plan_ref[me * slots + slot]
        due = due_ref[0, block]
        cost = cost_ref[0, block]
        factor_ref[slot] = jnp.ones((8, 128), F32)

        @pl.when(due <= 0)
        def _():
            copy = pltpu.make_async_copy(stale_ref.at[0, slot], root_ref.at[slot], stale_sem)
            copy.start()
            copy.wait()

        @pl.when(due > 0)
        def _():
            assemble(slot, block)
            total = jnp.zeros((8, order), F32)
            for start in range(0, order, 8):
                piece = full[start : start + 8, :]
                total = total + piece * piece
            norm = jnp.sqrt(jnp.full((8, 128), jnp.sum(total), F32))
            factor_ref[slot] = lax.rsqrt(norm)
            divisor = jnp.max(norm)
            for i, start in enumerate(range(0, order, chunk)):
                scaled = (full[rows[i], :] / divisor).astype(BF16)
                half_root[rows[i], :] = scaled
                root_ref[slot, rows[i], :] = (eye_rows(start) - 0.5 * scaled.astype(F32)).astype(
                    BF16
                )

            @pl.when(cost > 1)
            def _():
                first = [
                    jnp.dot(half_root[r, :], root_ref[slot], preferred_element_type=F32).astype(BF16)
                    for r in rows
                ]
                for r, value in zip(rows, first):
                    half_root[r, :] = value

                def correct():
                    for i, start in enumerate(range(0, order, chunk)):
                        product = jnp.dot(
                            root_ref[slot, rows[i], :], half_root[...], preferred_element_type=F32
                        )
                        correction[rows[i], :] = (eye_rows(start) - 0.5 * product).astype(BF16)

                def next_root():
                    values = [
                        jnp.dot(
                            correction[r, :], root_ref[slot], preferred_element_type=F32
                        ).astype(BF16)
                        for r in rows
                    ]
                    for r, value in zip(rows, values):
                        root_ref[slot, r, :] = value

                def sweep(step, carry):
                    correct()
                    values = [
                        jnp.dot(
                            half_root[r, :], correction[...], preferred_element_type=F32
                        ).astype(BF16)
                        for r in rows
                    ]
                    for r, value in zip(rows, values):
                        half_root[r, :] = value
                    next_root()
                    return carry

                lax.fori_loop(0, cost - 2, sweep, 0)
                correct()
                next_root()


def roots(plan, due, cost, stats, received, stale, slots):
    order = stats.shape[3]
    width = stats.shape[2]
    return call(
        functools.partial(root_kernel, slots),
        (
            jax.ShapeDtypeStruct((slots, order, order), BF16),
            jax.ShapeDtypeStruct((slots, 8, 128), F32),
        ),
        [IN_SMEM] * 3 + [ANYWHERE] + [IN_VMEM] * 3 + [ANYWHERE],
        (IN_VMEM, IN_VMEM),
        "roots",
        scratch=[
            pltpu.VMEM((width, order), BF16),
            pltpu.VMEM((order, order), F32),
            pltpu.VMEM((order, order), BF16),
            pltpu.VMEM((order, order), BF16),
            pltpu.SemaphoreType.DMA,
            pltpu.SemaphoreType.DMA,
        ],
        flops=slots * 9 * 2 * order**3,
        moved=slots * order * order * 6,
    )(plan, due, cost, stats, *received, stale)


def start_kernel(
    slots,
    plan_ref,
    root_ref,
    own_ref,
    grad1_ref,
    far_root_ref,
    near_root_ref,
    far_ref,
    near_ref,
    columns_ref,
):
    me = place_of(plan_ref)
    width = grad1_ref.shape[1]
    for slot in range(slots):
        here = jnp.concatenate([own_ref[slot], grad1_ref[slot]], axis=0)
        for places, root_out, out in (((2, 3), far_root_ref, far_ref), ((0, 1), near_root_ref, near_ref)):
            for i, row in enumerate(places):
                rows = tile_at(me ^ row, width)
                for j in range(2):
                    at = (slice(i * width, (i + 1) * width), slice(j * width, (j + 1) * width))
                    root_out[slot, at[0], at[1]] = root_ref[slot, rows, tile_at(me ^ (2 + j), width)]
                    columns_ref[at[0], at[1]] = root_ref[slot, rows, tile_at(me ^ j, width)]
            out[slot] = jnp.dot(columns_ref[...], here, preferred_element_type=F32)


def start_product(plan, root, own_grad, grad1):
    slots, width, columns = grad1.shape
    pair = jax.ShapeDtypeStruct((slots, 2 * width, 2 * width), BF16)
    total = jax.ShapeDtypeStruct((slots, 2 * width, columns), F32)
    return call(
        functools.partial(start_kernel, slots),
        (pair, pair, total, total),
        [IN_SMEM] + [IN_VMEM] * 3,
        (IN_VMEM,) * 4,
        "start_product",
        scratch=[pltpu.VMEM((2 * width, 2 * width), BF16)],
        flops=slots * 16 * width * width * columns,
        moved=slots * 16 * width * columns,
    )(plan, root, own_grad, grad1)


def finish_kernel(root_ref, begun_ref, factor_ref, grad3_ref, grad2_ref, *rest):
    first_ref, second_ref = rest[-2:] if len(rest) == 2 else rest[-3:-1]
    slots, width, columns = first_ref.shape
    total = jnp.zeros((8, 128), F32)
    for slot in range(slots):
        there = jnp.concatenate([grad2_ref[slot], grad3_ref[slot]], axis=0)
        product = begun_ref[slot] + jnp.dot(root_ref[slot], there, preferred_element_type=F32)
        rounded = (product * factor_ref[slot, :1, :1]).astype(BF16)
        first_ref[slot] = rounded[:width, :]
        second_ref[slot] = rounded[width:, :]
    if len(rest) > 2:
        own_ref, grad1_ref, out2_ref, out3_ref = rest[:4]
        for slot in range(slots):
            for result_ref, with_ref in (
                (first_ref, own_ref),
                (second_ref, grad1_ref),
                (out2_ref, grad2_ref),
                (out3_ref, grad3_ref),
            ):
                terms = result_ref[slot].astype(F32) * with_ref[slot].astype(F32)
                for start in range(0, width, 8):
                    for column in range(0, columns, 128):
                        total = total + terms[start : start + 8, column : column + 128]
        rest[-1][...] = total


def finish_product(root, begun, factor, grad2, grad3, *others):
    slots, width, columns = grad2.shape
    out = jax.ShapeDtypeStruct(grad2.shape, BF16)
    shapes = (out, out) + ((jax.ShapeDtypeStruct((8, 128), F32),) if others else ())
    return call(
        finish_kernel,
        shapes,
        [IN_VMEM] * (5 + len(others)),
        (IN_VMEM,) * len(shapes),
        "near_product" if others else "far_product",
        flops=slots * 8 * width * width * columns,
        moved=slots * 16 * width * columns,
    )(root, begun, factor, grad3, grad2, *others)


def clip_kernel(slots, elements, plan_ref, *rest):
    sums, rows, out_hbm, out_ref, sems = rest[:4], rest[4:8], *rest[8:]
    me = place_of(plan_ref)
    quadratic = jnp.sum(sums[0][...] + sums[1][...] + sums[2][...] + sums[3][...])
    ratio = jnp.full((8, 128), F32(KL_BOUND * elements)) / quadratic
    clip_factor = jnp.max(jnp.minimum(F32(1.0), jnp.sqrt(ratio)))
    copies = []
    for far in range(4):
        for slot in range(slots):
            at = far * slots + slot
            block = plan_ref[(me ^ far) * slots + slot]
            out_ref[at] = (clip_factor * rows[far][slot].astype(F32)).astype(BF16)
            copies.append(pltpu.make_async_copy(out_ref.at[at], out_hbm.at[0, block], sems.at[at]))
            copies[-1].start()
    for copy in copies:
        copy.wait()


def clip(plan, sums, rows, shape, slots, elements):
    return call(
        functools.partial(clip_kernel, slots, elements),
        jax.ShapeDtypeStruct(shape, BF16),
        [IN_SMEM] + [IN_VMEM] * (len(sums) + len(rows)),
        ANYWHERE,
        "clip",
        scratch=[pltpu.VMEM(shape[1:], BF16), pltpu.SemaphoreType.DMA((shape[1],))],
        moved=4 * shape[1] * shape[2] * shape[3],
    )(plan, *sums, *rows)


def after_kernel(value_ref, landed_ref, out_ref):
    out_ref[...] = value_ref[...]


def after(value, landed):
    return call(
        after_kernel,
        jax.ShapeDtypeStruct(value.shape, value.dtype),
        [IN_VMEM, ANYWHERE],
        IN_VMEM,
        "after",
    )(value, landed)


def partner_of(value, axis, far):
    count = lax.axis_size(axis)
    return lax.ppermute(value, axis, [(i, i ^ far) for i in range(count)])


def sum_over(value, axis):
    count = lax.axis_size(axis)
    total = value
    for shift in range(1, count):
        total = total + lax.ppermute(
            value, axis, [(i, (i + shift) % count) for i in range(count)]
        )
    return total


def exchange_four(stats, grad, due, cost, assign, stale):
    slots = assign.shape[1] // 4
    me = lax.axis_index("fsdp").astype(jnp.int32)
    plan = plan_of(assign[0], me)
    near, far2, far3 = pack_stats(me.reshape(1), assign, stats, slots)
    received = [partner_of(near, "fsdp", 1), partner_of(far3, "fsdp", 3), partner_of(far2, "fsdp", 2)]
    own_grad, *sent = pack_grad(plan, grad, slots)
    grad1, grad2, grad3 = [partner_of(piece, "fsdp", far) for far, piece in enumerate(sent, 1)]
    root, factor = roots(plan, due, cost, stats, received, stale, slots)
    far_root, near_root, far, near = start_product(plan, root, own_grad, grad1)
    out2, out3 = finish_product(far_root, far, factor, grad2, grad3)
    own, out1, total = finish_product(
        near_root, near, factor, grad2, grad3, own_grad, grad1, out2, out3
    )
    rows = [own] + [partner_of(out, "fsdp", far) for far, out in enumerate((out1, out2, out3), 1)]
    total = sum_over(total, "dp")
    sums = [total, partner_of(after(total, rows[3]), "fsdp", 1)]
    sums += [partner_of(total, "fsdp", far) for far in (2, 3)]
    elements = lax.axis_size("dp") * assign.shape[1] * stats.shape[3] * grad.shape[3]
    return clip(plan, sums, rows, grad.shape, slots, elements)


def solution(mesh):
    return jax.shard_map(
        exchange_four if mesh.shape["fsdp"] == 4 else exchange_all,
        mesh=mesh,
        in_specs=(
            P(("groups", "dp"), None, "fsdp", None),
            P(("groups", "dp"), None, "fsdp", None),
            P(("groups", "dp"), None),
            P(("groups", "dp"), None),
            P(("groups", "dp"), None),
            P(("groups", "dp"), "fsdp", None, None),
        ),
        out_specs=P(("groups", "dp"), None, "fsdp", None),
        check_vma=False,
    )
```

```python
import functools

import jax
import jax.numpy as jnp
from jax import lax
from jax.experimental import pallas as pl
from jax.experimental.pallas import tpu as pltpu
from jax.sharding import PartitionSpec as P

KL_BOUND = 1.0
VMEM_BYTES = 40 * 2**20
DIAGONAL_ROWS = 16
F32 = jnp.float32
BF16 = jnp.bfloat16


def refresh(block_piece, grad_rows, old_root, due_flag, sweep_count):
    full_block = block_piece.astype(F32)
    frobenius = jnp.sqrt(jnp.sum(full_block * full_block))
    identity = jnp.eye(full_block.shape[0], dtype=F32)
    root_half = (full_block / frobenius).astype(BF16)
    root_inverse = identity.astype(BF16)

    def sweep(step_index, iterates):
        half_now, inverse_now = iterates
        product = jnp.dot(inverse_now, half_now, preferred_element_type=F32)
        correction = (1.5 * identity - 0.5 * product).astype(BF16)
        half_next = jnp.dot(half_now, correction, preferred_element_type=F32).astype(BF16)
        inverse_next = jnp.dot(correction, inverse_now, preferred_element_type=F32).astype(BF16)
        return (half_next, inverse_next)

    root_half, root_inverse = lax.fori_loop(0, sweep_count, sweep, (root_half, root_inverse))
    left_factor = jnp.where(due_flag > 0, root_inverse, old_root)
    factor = jnp.where(due_flag > 0, lax.rsqrt(frobenius), F32(1.0))
    return (jnp.dot(left_factor, grad_rows, preferred_element_type=F32) * factor).astype(BF16)


def exchange_all(stats, grad, due, cost, assign, stale):
    own_index = lax.axis_index("fsdp")
    solver_count = lax.axis_size("fsdp")
    dp_count = lax.axis_size("dp")
    table_row = assign[0]
    due_row = due[0]
    cost_row = cost[0]
    total_slots = table_row.shape[0]
    slot_count = total_slots // solver_count
    row_count = stats.shape[2]
    block_order = stats.shape[3]
    column_count = grad.shape[3]
    source = jnp.argsort(table_row, stable=True)
    sent_stats = jnp.take(stats[0], source, axis=0).reshape(
        solver_count, slot_count, row_count, block_order
    )
    sent_grad = jnp.take(grad[0], source, axis=0).reshape(
        solver_count, slot_count, row_count, column_count
    )
    blocks_here, grads_here = (
        lax.all_to_all(sent_stats, "fsdp", split_axis=0, concat_axis=2, tiled=True),
        lax.all_to_all(sent_grad, "fsdp", split_axis=0, concat_axis=2, tiled=True),
    )
    my_blocks = lax.dynamic_slice_in_dim(source, own_index * slot_count, slot_count)
    results = []
    for slot in range(slot_count):
        block_id = my_blocks[slot]
        due_flag = due_row[block_id]
        results.append(
            refresh(
                blocks_here[0, slot],
                grads_here[0, slot],
                stale[0, slot],
                due_flag,
                cost_row[block_id] * due_flag,
            )
        )
    solved = jnp.stack(results)
    returned = lax.all_to_all(
        solved.reshape(slot_count, solver_count, row_count, column_count),
        "fsdp",
        split_axis=1,
        concat_axis=0,
        tiled=True,
    )
    owner_rows = jnp.take(returned.reshape(total_slots, row_count, column_count), table_row, axis=0)
    local_part = jnp.sum(owner_rows.astype(F32) * grad[0].astype(F32))
    quadratic = lax.psum(local_part, ("fsdp", "dp"))
    elements = dp_count * total_slots * block_order * column_count
    clip_factor = jnp.minimum(F32(1.0), jnp.sqrt(KL_BOUND * elements / quadratic))
    return (clip_factor * owner_rows.astype(F32)).astype(BF16)[None]


def call(kernel, out_shape, in_specs, out_specs, name, scratch=(), flops=0, moved=0):
    return pl.pallas_call(
        kernel,
        out_shape=out_shape,
        in_specs=in_specs,
        out_specs=out_specs,
        scratch_shapes=list(scratch),
        compiler_params=pltpu.CompilerParams(vmem_limit_bytes=VMEM_BYTES),
        cost_estimate=pl.CostEstimate(flops=flops, bytes_accessed=moved, transcendentals=0),
        name=name,
    )


IN_VMEM = pl.BlockSpec(memory_space=pltpu.VMEM)
IN_SMEM = pl.BlockSpec(memory_space=pltpu.SMEM)
ANYWHERE = pl.BlockSpec(memory_space=pl.ANY)


def plan_of(table_row, place, slots):
    total = table_row.shape[0]
    entry = lax.broadcasted_iota(jnp.int32, (total + 1, total), 0)
    wanted = (place ^ (entry // slots)) * slots + entry % slots
    blocks = lax.broadcasted_iota(jnp.int32, (total + 1, total), 1)
    source = jnp.sum(jnp.where(table_row[None, :] == wanted, blocks, 0), axis=1)
    return jnp.where(jnp.arange(total + 1) == total, place, source)


def place_of(plan_ref):
    return plan_ref[plan_ref.shape[0] - 1]


def tile_at(index, width):
    return pl.ds(pl.multiple_of(index * width, width), width)


def fold(tile):
    half = tile.shape[0] // 2
    row = lax.broadcasted_iota(jnp.int32, (half, 2 * half), 0)
    lane = lax.broadcasted_iota(jnp.int32, (half, 2 * half), 1)
    top, bottom = tile[:half, :], tile[half:, :]
    folded = jnp.where((lane < half) & (row > lane), pltpu.roll(bottom, half, 1), top)
    diagonal = jnp.sum(jnp.where(lane - half == row, bottom, 0.0), axis=0, keepdims=True)
    return folded, diagonal


def unfold(folded, diagonal):
    half = folded.shape[0]
    row = lax.broadcasted_iota(jnp.int32, (half, 2 * half), 0)
    lane = lax.broadcasted_iota(jnp.int32, (half, 2 * half), 1)
    turned = jnp.concatenate([folded, jnp.zeros_like(folded)], axis=0).T
    top = jnp.where((lane < half) & (row > lane), turned[:half, :], folded)
    last = jnp.where(
        lane - half < row,
        pltpu.roll(folded, half, 1),
        jnp.where(lane - half > row, pltpu.roll(turned[:half, :], half, 1), diagonal),
    )
    return jnp.concatenate([top, jnp.where(lane < half, turned[half:, :], last)], axis=0)


def block_in_slot(assign_ref, slot):
    found = jnp.int32(0)
    for block in range(assign_ref.shape[1]):
        found = jnp.where(assign_ref[0, block] == slot, jnp.int32(block), found)
    return found


def pack_stats_kernel(
    slots, me_ref, assign_hbm, stats_hbm, near_ref, far2_ref, far3_ref, assign_ref, stats_ref, sems
):
    blocks = stats_ref.shape[1]
    table = pltpu.make_async_copy(assign_hbm, assign_ref, sems.at[blocks])
    table.start()
    copies = [
        pltpu.make_async_copy(stats_hbm.at[0, block], stats_ref.at[0, block], sems.at[block])
        for block in range(blocks)
    ]
    for copy in copies:
        copy.start()
    me = me_ref[0]
    width = stats_ref.shape[2]
    table.wait()
    for copy in copies:
        copy.wait()
    half = width // 2
    odd = me % 2
    for far, out in ((2, far2_ref), (3, far3_ref)):
        diagonals = []
        for slot in range(slots):
            block = block_in_slot(assign_ref, (me ^ far) * slots + slot)
            between = stats_ref[0, block, :, tile_at(me ^ 1, width)].astype(F32)
            at = slot * width
            out[at : at + half, :] = jnp.where(
                odd == 1, between.T[half:, :], between[:half, :]
            ).astype(BF16)
            folded, diagonal = fold(stats_ref[0, block, :, tile_at(me, width)].astype(F32))
            out[at + half : at + width, :] = folded.astype(BF16)
            diagonals.append(diagonal)
        lane = lax.broadcasted_iota(jnp.int32, (1, width), 1)
        for start in range(0, slots, 2):
            pair = pltpu.roll(diagonals[start], half, 1)
            if start + 1 < slots:
                pair = jnp.where(lane < half, pair, diagonals[start + 1])
            at = slots * width + start // 2 * DIAGONAL_ROWS
            out[at : at + DIAGONAL_ROWS, :] = jnp.broadcast_to(pair, (DIAGONAL_ROWS, width)).astype(
                BF16
            )
    for slot in range(slots):
        block = block_in_slot(assign_ref, (me ^ 1) * slots + slot)
        for place, other in enumerate((0, 2, 3)):
            near_ref[slot, :, place * width : (place + 1) * width] = stats_ref[
                0, block, :, tile_at(me ^ other, width)
            ]


def pack_stats(me, assign, stats, slots):
    width, order = stats.shape[2:]
    near = jax.ShapeDtypeStruct((slots, width, order - width), BF16)
    far = jax.ShapeDtypeStruct((slots * width + (slots + 1) // 2 * DIAGONAL_ROWS, width), BF16)
    return call(
        functools.partial(pack_stats_kernel, slots),
        (near, far, far),
        [IN_SMEM, ANYWHERE, ANYWHERE],
        (IN_VMEM,) * 3,
        "pack_stats",
        scratch=[
            pltpu.SMEM(assign.shape, jnp.int32),
            pltpu.VMEM(stats.shape, BF16),
            pltpu.SemaphoreType.DMA((stats.shape[1] + 1,)),
        ],
        moved=2 * stats.size * 2,
    )(me, *(pltpu.with_memory_space_constraint(x, pltpu.HBM) for x in (assign, stats)))


def pack_grad_kernel(slots, plan_ref, grad_ref, *outs):
    for far in (3, 2, 1, 0):
        for slot in range(slots):
            outs[far][slot] = grad_ref[0, plan_ref[far * slots + slot]]


def pack_grad(plan, grad, slots):
    out = jax.ShapeDtypeStruct((slots, *grad.shape[2:]), BF16)
    return call(
        functools.partial(pack_grad_kernel, slots),
        (out,) * 4,
        [IN_SMEM, IN_VMEM],
        (IN_VMEM,) * 4,
        "pack_grad",
        moved=2 * grad.size * 2,
    )(plan, grad)


def root_kernel(
    slots,
    plan_ref,
    due_ref,
    cost_ref,
    stats_ref,
    near_ref,
    far3_ref,
    far2_ref,
    stale_ref,
    root_ref,
    factor_ref,
    own,
    full,
    half_root,
    correction,
    sem,
    stale_sem,
):
    me = place_of(plan_ref)
    order = full.shape[0]
    width = near_ref.shape[1]
    half = width // 2
    chunk = order // 2
    rows = [pl.ds(start, chunk) for start in range(0, order, chunk)]

    def eye_rows(start):
        r = lax.broadcasted_iota(jnp.int32, (chunk, order), 0) + start
        c = lax.broadcasted_iota(jnp.int32, (chunk, order), 1)
        return jnp.where(r == c, F32(1.5), F32(0.0))

    def assemble(slot, block):
        copy = pltpu.make_async_copy(stats_ref.at[0, block], own, sem)
        copy.start()
        even, odd = (me ^ 2) & 2, ((me ^ 2) & 2) + 1
        at = lambda index: tile_at(index, width)
        two, three = me ^ 2, me ^ 3
        start = slot * width
        row = slots * width + slot // 2 * DIAGONAL_ROWS
        for index, far_ref in ((two, far2_ref), (three, far3_ref)):
            diagonal = far_ref[row : row + 8, :].astype(F32)
            if slot % 2 == 0:
                diagonal = pltpu.roll(diagonal, half, 1)
            full[at(index), at(index)] = unfold(
                far_ref[start + half : start + width, :].astype(F32), diagonal[:1, :]
            )
        from_two = far2_ref[start : start + half, :].astype(F32)
        from_three = far3_ref[start : start + half, :].astype(F32)
        two_is_even = me % 2 == 0
        between = jnp.concatenate(
            [
                jnp.where(two_is_even, from_two, from_three),
                jnp.where(two_is_even, from_three, from_two),
            ],
            axis=0,
        )
        full[at(even), at(odd)] = between
        full[at(odd), at(even)] = between.T
        near = me ^ 1
        for place, other in enumerate((0, 2, 3)):
            tile = near_ref[slot, :, place * width : (place + 1) * width].astype(F32)
            full[at(near), at(near ^ other)] = tile
            if other:
                full[at(near ^ other), at(near)] = tile.T
        copy.wait()
        full[at(me), :] = own[...].astype(F32)
        for other in (1, 2, 3):
            full[at(me ^ other), at(me)] = own[:, at(me ^ other)].astype(F32).T

    for slot in range(slots):
        block = plan_ref[slot]
        due = due_ref[0, block]
        cost = cost_ref[0, block]
        factor_ref[slot] = jnp.ones((8, 128), F32)

        @pl.when(due <= 0)
        def _():
            copy = pltpu.make_async_copy(stale_ref.at[0, slot], root_ref.at[slot], stale_sem)
            copy.start()
            copy.wait()

        @pl.when(due > 0)
        def _():
            assemble(slot, block)
            total = jnp.zeros((8, order), F32)
            for start in range(0, order, 8):
                piece = full[start : start + 8, :]
                total = total + piece * piece
            norm = jnp.sqrt(jnp.full((8, 128), jnp.sum(total), F32))
            factor_ref[slot] = lax.rsqrt(norm)
            divisor = jnp.max(norm)
            for i, start in enumerate(range(0, order, chunk)):
                scaled = (full[rows[i], :] / divisor).astype(BF16)
                half_root[rows[i], :] = scaled
                root_ref[slot, rows[i], :] = (eye_rows(start) - 0.5 * scaled.astype(F32)).astype(
                    BF16
                )

            @pl.when(cost > 1)
            def _():
                first = [
                    jnp.dot(half_root[r, :], root_ref[slot], preferred_element_type=F32).astype(BF16)
                    for r in rows
                ]
                for r, value in zip(rows, first):
                    half_root[r, :] = value

                def correct():
                    for i, start in enumerate(range(0, order, chunk)):
                        product = jnp.dot(
                            root_ref[slot, rows[i], :], half_root[...], preferred_element_type=F32
                        )
                        correction[rows[i], :] = (eye_rows(start) - 0.5 * product).astype(BF16)

                def next_root():
                    values = [
                        jnp.dot(
                            correction[r, :], root_ref[slot], preferred_element_type=F32
                        ).astype(BF16)
                        for r in rows
                    ]
                    for r, value in zip(rows, values):
                        root_ref[slot, r, :] = value

                def sweep(step, carry):
                    correct()
                    values = [
                        jnp.dot(
                            half_root[r, :], correction[...], preferred_element_type=F32
                        ).astype(BF16)
                        for r in rows
                    ]
                    for r, value in zip(rows, values):
                        half_root[r, :] = value
                    next_root()
                    return carry

                lax.fori_loop(0, cost - 2, sweep, 0)
                correct()
                next_root()


def roots(plan, due, cost, stats, received, stale, slots):
    order = stats.shape[3]
    width = stats.shape[2]
    return call(
        functools.partial(root_kernel, slots),
        (
            jax.ShapeDtypeStruct((slots, order, order), BF16),
            jax.ShapeDtypeStruct((slots, 8, 128), F32),
        ),
        [IN_SMEM] * 3 + [ANYWHERE] + [IN_VMEM] * 3 + [ANYWHERE],
        (IN_VMEM, IN_VMEM),
        "roots",
        scratch=[
            pltpu.VMEM((width, order), BF16),
            pltpu.VMEM((order, order), F32),
            pltpu.VMEM((order, order), BF16),
            pltpu.VMEM((order, order), BF16),
            pltpu.SemaphoreType.DMA,
            pltpu.SemaphoreType.DMA,
        ],
        flops=slots * 9 * 2 * order**3,
        moved=slots * order * order * 6,
    )(plan, due, cost, stats, *received, stale)


def start_kernel(
    slots,
    plan_ref,
    root_ref,
    own_ref,
    grad1_ref,
    far_root_ref,
    near_root_ref,
    far_ref,
    near_ref,
    columns_ref,
):
    me = place_of(plan_ref)
    width = grad1_ref.shape[1]
    for slot in range(slots):
        here = jnp.concatenate([own_ref[slot], grad1_ref[slot]], axis=0)
        for places, root_out, out in (((2, 3), far_root_ref, far_ref), ((0, 1), near_root_ref, near_ref)):
            for i, row in enumerate(places):
                rows = tile_at(me ^ row, width)
                for j in range(2):
                    at = (slice(i * width, (i + 1) * width), slice(j * width, (j + 1) * width))
                    root_out[slot, at[0], at[1]] = root_ref[slot, rows, tile_at(me ^ (2 + j), width)]
                    columns_ref[at[0], at[1]] = root_ref[slot, rows, tile_at(me ^ j, width)]
            out[slot] = jnp.dot(columns_ref[...], here, preferred_element_type=F32)


def start_product(plan, root, own_grad, grad1):
    slots, width, columns = grad1.shape
    pair = jax.ShapeDtypeStruct((slots, 2 * width, 2 * width), BF16)
    total = jax.ShapeDtypeStruct((slots, 2 * width, columns), F32)
    return call(
        functools.partial(start_kernel, slots),
        (pair, pair, total, total),
        [IN_SMEM] + [IN_VMEM] * 3,
        (IN_VMEM,) * 4,
        "start_product",
        scratch=[pltpu.VMEM((2 * width, 2 * width), BF16)],
        flops=slots * 16 * width * width * columns,
        moved=slots * 16 * width * columns,
    )(plan, root, own_grad, grad1)


def finish_kernel(root_ref, begun_ref, factor_ref, grad3_ref, grad2_ref, *rest):
    first_ref, second_ref = rest[-2:] if len(rest) == 2 else rest[-3:-1]
    slots, width, columns = first_ref.shape
    total = jnp.zeros((8, 128), F32)
    for slot in range(slots):
        there = jnp.concatenate([grad2_ref[slot], grad3_ref[slot]], axis=0)
        product = begun_ref[slot] + jnp.dot(root_ref[slot], there, preferred_element_type=F32)
        rounded = (product * factor_ref[slot, :1, :1]).astype(BF16)
        first_ref[slot] = rounded[:width, :]
        second_ref[slot] = rounded[width:, :]
    if len(rest) > 2:
        own_ref, grad1_ref, out2_ref, out3_ref = rest[:4]
        for slot in range(slots):
            for result_ref, with_ref in (
                (first_ref, own_ref),
                (second_ref, grad1_ref),
                (out2_ref, grad2_ref),
                (out3_ref, grad3_ref),
            ):
                terms = result_ref[slot].astype(F32) * with_ref[slot].astype(F32)
                for start in range(0, width, 8):
                    for column in range(0, columns, 128):
                        total = total + terms[start : start + 8, column : column + 128]
        rest[-1][...] = jnp.sum(total, axis=0, keepdims=True)


def finish_product(root, begun, factor, grad2, grad3, *others):
    slots, width, columns = grad2.shape
    out = jax.ShapeDtypeStruct(grad2.shape, BF16)
    shapes = (out, out) + ((jax.ShapeDtypeStruct((1, 128), F32),) if others else ())
    return call(
        finish_kernel,
        shapes,
        [IN_VMEM] * (5 + len(others)),
        (IN_VMEM,) * len(shapes),
        "near_product" if others else "far_product",
        flops=slots * 8 * width * width * columns,
        moved=slots * 16 * width * columns,
    )(root, begun, factor, grad3, grad2, *others)


def clip_kernel(slots, elements, plan_ref, *rest):
    sums, rows, out_hbm, out_ref, sems = rest[:4], rest[4:8], *rest[8:]
    plan = plan_ref[...]
    entry = lax.broadcasted_iota(jnp.int32, plan.shape, 1)
    blocks = [jnp.sum(jnp.where(entry == at, plan, 0)) for at in range(4 * slots)]
    lanes = sums[0][...] + sums[1][...] + sums[2][...] + sums[3][...]
    quadratic = jnp.sum(lanes, axis=1, keepdims=True)
    clip_factor = jnp.minimum(F32(1.0), jnp.sqrt(F32(KL_BOUND * elements) / quadratic))
    copies = []
    for far in range(4):
        for slot in range(slots):
            at = far * slots + slot
            out_ref[at] = (clip_factor * rows[far][slot].astype(F32)).astype(BF16)
            copies.append(
                pltpu.make_async_copy(out_ref.at[at], out_hbm.at[0, blocks[at]], sems.at[at])
            )
            copies[-1].start()
    for copy in copies:
        copy.wait()


def clip(plan, sums, rows, shape, slots, elements):
    return call(
        functools.partial(clip_kernel, slots, elements),
        jax.ShapeDtypeStruct(shape, BF16),
        [IN_VMEM] * (1 + len(sums) + len(rows)),
        ANYWHERE,
        "clip",
        scratch=[pltpu.VMEM(shape[1:], BF16), pltpu.SemaphoreType.DMA((shape[1],))],
        moved=4 * shape[1] * shape[2] * shape[3],
    )(plan[None], *sums, *rows)


def after_kernel(value_ref, landed_ref, out_ref):
    out_ref[...] = value_ref[...]


def after(value, landed):
    return call(
        after_kernel,
        jax.ShapeDtypeStruct(value.shape, value.dtype),
        [IN_VMEM, ANYWHERE],
        IN_VMEM,
        "after",
    )(value, landed)


def partner_of(value, axis, far):
    count = lax.axis_size(axis)
    return lax.ppermute(value, axis, [(i, i ^ far) for i in range(count)])


def sum_over(value, axis):
    count = lax.axis_size(axis)
    total = value
    for shift in range(1, count):
        total = total + lax.ppermute(
            value, axis, [(i, (i + shift) % count) for i in range(count)]
        )
    return total


def exchange_four(stats, grad, due, cost, assign, stale):
    slots = assign.shape[1] // 4
    me = lax.axis_index("fsdp").astype(jnp.int32)
    plan = plan_of(assign[0], me, slots)
    near, far2, far3 = pack_stats(me.reshape(1), assign, stats, slots)
    received = [partner_of(near, "fsdp", 1), partner_of(far3, "fsdp", 3), partner_of(far2, "fsdp", 2)]
    own_grad, *sent = pack_grad(plan, grad, slots)
    grad1, grad2, grad3 = [partner_of(piece, "fsdp", far) for far, piece in enumerate(sent, 1)]
    root, factor = roots(plan, due, cost, stats, received, stale, slots)
    far_root, near_root, far, near = start_product(plan, root, own_grad, grad1)
    out2, out3 = finish_product(far_root, far, factor, grad2, grad3)
    own, out1, total = finish_product(
        near_root, near, factor, grad2, grad3, own_grad, grad1, out2, out3
    )
    rows = [own] + [partner_of(out, "fsdp", far) for far, out in enumerate((out1, out2, out3), 1)]
    total = sum_over(total, "dp")
    sums = [total, partner_of(after(total, rows[3]), "fsdp", 1)]
    sums += [partner_of(total, "fsdp", far) for far in (2, 3)]
    elements = lax.axis_size("dp") * assign.shape[1] * stats.shape[3] * grad.shape[3]
    return clip(plan, sums, rows, grad.shape, slots, elements)


def solution(mesh):
    return jax.shard_map(
        exchange_four if mesh.shape["fsdp"] == 4 else exchange_all,
        mesh=mesh,
        in_specs=(
            P(("groups", "dp"), None, "fsdp", None),
            P(("groups", "dp"), None, "fsdp", None),
            P(("groups", "dp"), None),
            P(("groups", "dp"), None),
            P(("groups", "dp"), None),
            P(("groups", "dp"), "fsdp", None, None),
        ),
        out_specs=P(("groups", "dp"), None, "fsdp", None),
        check_vma=False,
    )
```

```python
import functools

import jax
import jax.numpy as jnp
from jax import lax
from jax.experimental import pallas as pl
from jax.experimental.pallas import tpu as pltpu
from jax.sharding import PartitionSpec as P

KL_BOUND = 1.0
VMEM_BYTES = 40 * 2**20
DIAGONAL_ROWS = 16
F32 = jnp.float32
BF16 = jnp.bfloat16


def refresh(block_piece, grad_rows, old_root, due_flag, sweep_count):
    full_block = block_piece.astype(F32)
    frobenius = jnp.sqrt(jnp.sum(full_block * full_block))
    identity = jnp.eye(full_block.shape[0], dtype=F32)
    root_half = (full_block / frobenius).astype(BF16)
    root_inverse = identity.astype(BF16)

    def sweep(step_index, iterates):
        half_now, inverse_now = iterates
        product = jnp.dot(inverse_now, half_now, preferred_element_type=F32)
        correction = (1.5 * identity - 0.5 * product).astype(BF16)
        half_next = jnp.dot(half_now, correction, preferred_element_type=F32).astype(BF16)
        inverse_next = jnp.dot(correction, inverse_now, preferred_element_type=F32).astype(BF16)
        return (half_next, inverse_next)

    root_half, root_inverse = lax.fori_loop(0, sweep_count, sweep, (root_half, root_inverse))
    left_factor = jnp.where(due_flag > 0, root_inverse, old_root)
    factor = jnp.where(due_flag > 0, lax.rsqrt(frobenius), F32(1.0))
    return (jnp.dot(left_factor, grad_rows, preferred_element_type=F32) * factor).astype(BF16)


def exchange_all(stats, grad, due, cost, assign, stale):
    own_index = lax.axis_index("fsdp")
    solver_count = lax.axis_size("fsdp")
    dp_count = lax.axis_size("dp")
    table_row = assign[0]
    due_row = due[0]
    cost_row = cost[0]
    total_slots = table_row.shape[0]
    slot_count = total_slots // solver_count
    row_count = stats.shape[2]
    block_order = stats.shape[3]
    column_count = grad.shape[3]
    source = jnp.argsort(table_row, stable=True)
    sent_stats = jnp.take(stats[0], source, axis=0).reshape(
        solver_count, slot_count, row_count, block_order
    )
    sent_grad = jnp.take(grad[0], source, axis=0).reshape(
        solver_count, slot_count, row_count, column_count
    )
    blocks_here, grads_here = (
        lax.all_to_all(sent_stats, "fsdp", split_axis=0, concat_axis=2, tiled=True),
        lax.all_to_all(sent_grad, "fsdp", split_axis=0, concat_axis=2, tiled=True),
    )
    my_blocks = lax.dynamic_slice_in_dim(source, own_index * slot_count, slot_count)
    results = []
    for slot in range(slot_count):
        block_id = my_blocks[slot]
        due_flag = due_row[block_id]
        results.append(
            refresh(
                blocks_here[0, slot],
                grads_here[0, slot],
                stale[0, slot],
                due_flag,
                cost_row[block_id] * due_flag,
            )
        )
    solved = jnp.stack(results)
    returned = lax.all_to_all(
        solved.reshape(slot_count, solver_count, row_count, column_count),
        "fsdp",
        split_axis=1,
        concat_axis=0,
        tiled=True,
    )
    owner_rows = jnp.take(returned.reshape(total_slots, row_count, column_count), table_row, axis=0)
    local_part = jnp.sum(owner_rows.astype(F32) * grad[0].astype(F32))
    quadratic = lax.psum(local_part, ("fsdp", "dp"))
    elements = dp_count * total_slots * block_order * column_count
    clip_factor = jnp.minimum(F32(1.0), jnp.sqrt(KL_BOUND * elements / quadratic))
    return (clip_factor * owner_rows.astype(F32)).astype(BF16)[None]


def call(kernel, out_shape, in_specs, out_specs, name, scratch=(), flops=0, moved=0):
    return pl.pallas_call(
        kernel,
        out_shape=out_shape,
        in_specs=in_specs,
        out_specs=out_specs,
        scratch_shapes=list(scratch),
        compiler_params=pltpu.CompilerParams(vmem_limit_bytes=VMEM_BYTES),
        cost_estimate=pl.CostEstimate(flops=flops, bytes_accessed=moved, transcendentals=0),
        name=name,
    )


IN_VMEM = pl.BlockSpec(memory_space=pltpu.VMEM)
IN_SMEM = pl.BlockSpec(memory_space=pltpu.SMEM)
ANYWHERE = pl.BlockSpec(memory_space=pl.ANY)


def plan_of(table_row, place, slots):
    total = table_row.shape[0]
    entry = lax.broadcasted_iota(jnp.int32, (total + 1, total), 0)
    wanted = (place ^ (entry // slots)) * slots + entry % slots
    blocks = lax.broadcasted_iota(jnp.int32, (total + 1, total), 1)
    source = jnp.sum(jnp.where(table_row[None, :] == wanted, blocks, 0), axis=1)
    return jnp.where(jnp.arange(total + 1) == total, place, source)


def place_of(plan_ref):
    return plan_ref[plan_ref.shape[0] - 1]


def tile_at(index, width):
    return pl.ds(pl.multiple_of(index * width, width), width)


def fold(tile):
    half = tile.shape[0] // 2
    row = lax.broadcasted_iota(jnp.int32, (half, 2 * half), 0)
    lane = lax.broadcasted_iota(jnp.int32, (half, 2 * half), 1)
    top, bottom = tile[:half, :], tile[half:, :]
    folded = jnp.where((lane < half) & (row > lane), pltpu.roll(bottom, half, 1), top)
    diagonal = jnp.sum(jnp.where(lane - half == row, bottom, 0.0), axis=0, keepdims=True)
    return folded, diagonal


def unfold(folded, diagonal):
    half = folded.shape[0]
    row = lax.broadcasted_iota(jnp.int32, (half, 2 * half), 0)
    lane = lax.broadcasted_iota(jnp.int32, (half, 2 * half), 1)
    turned = jnp.concatenate([folded, jnp.zeros_like(folded)], axis=0).T
    top = jnp.where((lane < half) & (row > lane), turned[:half, :], folded)
    last = jnp.where(
        lane - half < row,
        pltpu.roll(folded, half, 1),
        jnp.where(lane - half > row, pltpu.roll(turned[:half, :], half, 1), diagonal),
    )
    return jnp.concatenate([top, jnp.where(lane < half, turned[half:, :], last)], axis=0)


def block_in_slot(assign_ref, slot):
    found = jnp.int32(0)
    for block in range(assign_ref.shape[1]):
        found = jnp.where(assign_ref[0, block] == slot, jnp.int32(block), found)
    return found


def pack_stats_kernel(
    slots, me_ref, assign_hbm, stats_hbm, near_ref, far2_ref, far3_ref, assign_ref, stats_ref, sems
):
    blocks = stats_ref.shape[1]
    table = pltpu.make_async_copy(assign_hbm, assign_ref, sems.at[blocks])
    table.start()
    copies = [
        pltpu.make_async_copy(stats_hbm.at[0, block], stats_ref.at[0, block], sems.at[block])
        for block in range(blocks)
    ]
    for copy in copies:
        copy.start()
    me = me_ref[0]
    width = stats_ref.shape[2]
    table.wait()
    for copy in copies:
        copy.wait()
    half = width // 2
    odd = me % 2
    for far, out in ((2, far2_ref), (3, far3_ref)):
        diagonals = []
        for slot in range(slots):
            block = block_in_slot(assign_ref, (me ^ far) * slots + slot)
            between = stats_ref[0, block, :, tile_at(me ^ 1, width)].astype(F32)
            at = slot * width
            out[at : at + half, :] = jnp.where(
                odd == 1, between.T[half:, :], between[:half, :]
            ).astype(BF16)
            folded, diagonal = fold(stats_ref[0, block, :, tile_at(me, width)].astype(F32))
            out[at + half : at + width, :] = folded.astype(BF16)
            diagonals.append(diagonal)
        lane = lax.broadcasted_iota(jnp.int32, (1, width), 1)
        for start in range(0, slots, 2):
            pair = pltpu.roll(diagonals[start], half, 1)
            if start + 1 < slots:
                pair = jnp.where(lane < half, pair, diagonals[start + 1])
            at = slots * width + start // 2 * DIAGONAL_ROWS
            out[at : at + DIAGONAL_ROWS, :] = jnp.broadcast_to(pair, (DIAGONAL_ROWS, width)).astype(
                BF16
            )
    for slot in range(slots):
        block = block_in_slot(assign_ref, (me ^ 1) * slots + slot)
        for place, other in enumerate((0, 2, 3)):
            near_ref[slot, :, place * width : (place + 1) * width] = stats_ref[
                0, block, :, tile_at(me ^ other, width)
            ]


def pack_stats(me, assign, stats, slots):
    width, order = stats.shape[2:]
    near = jax.ShapeDtypeStruct((slots, width, order - width), BF16)
    far = jax.ShapeDtypeStruct((slots * width + (slots + 1) // 2 * DIAGONAL_ROWS, width), BF16)
    return call(
        functools.partial(pack_stats_kernel, slots),
        (near, far, far),
        [IN_SMEM, ANYWHERE, ANYWHERE],
        (IN_VMEM,) * 3,
        "pack_stats",
        scratch=[
            pltpu.SMEM(assign.shape, jnp.int32),
            pltpu.VMEM(stats.shape, BF16),
            pltpu.SemaphoreType.DMA((stats.shape[1] + 1,)),
        ],
        moved=2 * stats.size * 2,
    )(me, *(pltpu.with_memory_space_constraint(x, pltpu.HBM) for x in (assign, stats)))


def pack_grad_kernel(slots, plan_ref, grad_ref, *outs):
    for far in (3, 2, 1, 0):
        for slot in range(slots):
            outs[far][slot] = grad_ref[0, plan_ref[far * slots + slot]]


def pack_grad(plan, grad, slots):
    out = jax.ShapeDtypeStruct((slots, *grad.shape[2:]), BF16)
    return call(
        functools.partial(pack_grad_kernel, slots),
        (out,) * 4,
        [IN_SMEM, IN_VMEM],
        (IN_VMEM,) * 4,
        "pack_grad",
        moved=2 * grad.size * 2,
    )(plan, grad)


def root_kernel(
    slots,
    plan_ref,
    due_ref,
    cost_ref,
    stats_ref,
    near_ref,
    far3_ref,
    far2_ref,
    stale_ref,
    root_ref,
    factor_ref,
    own,
    full,
    half_root,
    correction,
    sem,
    stale_sem,
):
    me = place_of(plan_ref)
    order = full.shape[0]
    width = near_ref.shape[1]
    half = width // 2
    chunk = order // 2
    rows = [pl.ds(start, chunk) for start in range(0, order, chunk)]

    def eye_rows(start):
        r = lax.broadcasted_iota(jnp.int32, (chunk, order), 0) + start
        c = lax.broadcasted_iota(jnp.int32, (chunk, order), 1)
        return jnp.where(r == c, F32(1.5), F32(0.0))

    def assemble(slot, block):
        copy = pltpu.make_async_copy(stats_ref.at[0, block], own, sem)
        copy.start()
        even, odd = (me ^ 2) & 2, ((me ^ 2) & 2) + 1
        at = lambda index: tile_at(index, width)
        two, three = me ^ 2, me ^ 3
        start = slot * width
        row = slots * width + slot // 2 * DIAGONAL_ROWS
        for index, far_ref in ((two, far2_ref), (three, far3_ref)):
            diagonal = far_ref[row : row + DIAGONAL_ROWS, :].astype(F32)
            if slot % 2 == 0:
                diagonal = pltpu.roll(diagonal, half, 1)
            full[at(index), at(index)] = unfold(
                far_ref[start + half : start + width, :].astype(F32), diagonal[:1, :]
            )
        from_two = far2_ref[start : start + half, :].astype(F32)
        from_three = far3_ref[start : start + half, :].astype(F32)
        two_is_even = me % 2 == 0
        between = jnp.concatenate(
            [
                jnp.where(two_is_even, from_two, from_three),
                jnp.where(two_is_even, from_three, from_two),
            ],
            axis=0,
        )
        full[at(even), at(odd)] = between
        full[at(odd), at(even)] = between.T
        near = me ^ 1
        for place, other in enumerate((0, 2, 3)):
            tile = near_ref[slot, :, place * width : (place + 1) * width].astype(F32)
            full[at(near), at(near ^ other)] = tile
            if other:
                full[at(near ^ other), at(near)] = tile.T
        copy.wait()
        full[at(me), :] = own[...].astype(F32)
        for other in (1, 2, 3):
            full[at(me ^ other), at(me)] = own[:, at(me ^ other)].astype(F32).T

    for slot in range(slots):
        block = plan_ref[slot]
        due = due_ref[0, block]
        cost = cost_ref[0, block]
        factor_ref[slot] = jnp.ones((8, 128), F32)

        @pl.when(due <= 0)
        def _():
            copy = pltpu.make_async_copy(stale_ref.at[0, slot], root_ref.at[slot], stale_sem)
            copy.start()
            copy.wait()

        @pl.when(due > 0)
        def _():
            assemble(slot, block)
            total = jnp.zeros((8, order), F32)
            for start in range(0, order, 8):
                piece = full[start : start + 8, :]
                total = total + piece * piece
            norm = jnp.sqrt(jnp.full((8, 128), jnp.sum(total), F32))
            factor_ref[slot] = lax.rsqrt(norm)
            divisor = jnp.max(norm)
            for i, start in enumerate(range(0, order, chunk)):
                scaled = (full[rows[i], :] / divisor).astype(BF16)
                half_root[rows[i], :] = scaled
                root_ref[slot, rows[i], :] = (eye_rows(start) - 0.5 * scaled.astype(F32)).astype(
                    BF16
                )

            @pl.when(cost > 1)
            def _():
                first = [
                    jnp.dot(half_root[r, :], root_ref[slot], preferred_element_type=F32).astype(BF16)
                    for r in rows
                ]
                for r, value in zip(rows, first):
                    half_root[r, :] = value

                def correct():
                    for i, start in enumerate(range(0, order, chunk)):
                        product = jnp.dot(
                            root_ref[slot, rows[i], :], half_root[...], preferred_element_type=F32
                        )
                        correction[rows[i], :] = (eye_rows(start) - 0.5 * product).astype(BF16)

                def next_root():
                    values = [
                        jnp.dot(
                            correction[r, :], root_ref[slot], preferred_element_type=F32
                        ).astype(BF16)
                        for r in rows
                    ]
                    for r, value in zip(rows, values):
                        root_ref[slot, r, :] = value

                def sweep(step, carry):
                    correct()
                    values = [
                        jnp.dot(
                            half_root[r, :], correction[...], preferred_element_type=F32
                        ).astype(BF16)
                        for r in rows
                    ]
                    for r, value in zip(rows, values):
                        half_root[r, :] = value
                    next_root()
                    return carry

                lax.fori_loop(0, cost - 2, sweep, 0)
                correct()
                next_root()


def roots(plan, due, cost, stats, received, stale, slots):
    order = stats.shape[3]
    width = stats.shape[2]
    return call(
        functools.partial(root_kernel, slots),
        (
            jax.ShapeDtypeStruct((slots, order, order), BF16),
            jax.ShapeDtypeStruct((slots, 8, 128), F32),
        ),
        [IN_SMEM] * 3 + [ANYWHERE] + [IN_VMEM] * 3 + [ANYWHERE],
        (IN_VMEM, IN_VMEM),
        "roots",
        scratch=[
            pltpu.VMEM((width, order), BF16),
            pltpu.VMEM((order, order), F32),
            pltpu.VMEM((order, order), BF16),
            pltpu.VMEM((order, order), BF16),
            pltpu.SemaphoreType.DMA,
            pltpu.SemaphoreType.DMA,
        ],
        flops=slots * 9 * 2 * order**3,
        moved=slots * order * order * 6,
    )(plan, due, cost, stats, *received, stale)


def start_kernel(
    slots,
    plan_ref,
    root_ref,
    own_ref,
    grad1_ref,
    far_root_ref,
    near_root_ref,
    far_ref,
    near_ref,
    columns_ref,
):
    me = place_of(plan_ref)
    width = grad1_ref.shape[1]
    for slot in range(slots):
        here = jnp.concatenate([own_ref[slot], grad1_ref[slot]], axis=0)
        for places, root_out, out in (((2, 3), far_root_ref, far_ref), ((0, 1), near_root_ref, near_ref)):
            for i, row in enumerate(places):
                rows = tile_at(me ^ row, width)
                for j in range(2):
                    at = (slice(i * width, (i + 1) * width), slice(j * width, (j + 1) * width))
                    root_out[slot, at[0], at[1]] = root_ref[slot, rows, tile_at(me ^ (2 + j), width)]
                    columns_ref[at[0], at[1]] = root_ref[slot, rows, tile_at(me ^ j, width)]
            out[slot] = jnp.dot(columns_ref[...], here, preferred_element_type=F32)


def start_product(plan, root, own_grad, grad1):
    slots, width, columns = grad1.shape
    pair = jax.ShapeDtypeStruct((slots, 2 * width, 2 * width), BF16)
    total = jax.ShapeDtypeStruct((slots, 2 * width, columns), F32)
    return call(
        functools.partial(start_kernel, slots),
        (pair, pair, total, total),
        [IN_SMEM] + [IN_VMEM] * 3,
        (IN_VMEM,) * 4,
        "start_product",
        scratch=[pltpu.VMEM((2 * width, 2 * width), BF16)],
        flops=slots * 16 * width * width * columns,
        moved=slots * 16 * width * columns,
    )(plan, root, own_grad, grad1)


def finish_kernel(root_ref, begun_ref, factor_ref, grad3_ref, grad2_ref, *rest):
    first_ref, second_ref = rest[-2:] if len(rest) == 2 else rest[-3:-1]
    slots, width, columns = first_ref.shape
    total = jnp.zeros((8, 128), F32)
    for slot in range(slots):
        there = jnp.concatenate([grad2_ref[slot], grad3_ref[slot]], axis=0)
        product = begun_ref[slot] + jnp.dot(root_ref[slot], there, preferred_element_type=F32)
        rounded = (product * factor_ref[slot, :1, :1]).astype(BF16)
        first_ref[slot] = rounded[:width, :]
        second_ref[slot] = rounded[width:, :]
    if len(rest) > 2:
        own_ref, grad1_ref, out2_ref, out3_ref = rest[:4]
        for slot in range(slots):
            for result_ref, with_ref in (
                (first_ref, own_ref),
                (second_ref, grad1_ref),
                (out2_ref, grad2_ref),
                (out3_ref, grad3_ref),
            ):
                terms = result_ref[slot].astype(F32) * with_ref[slot].astype(F32)
                for start in range(0, width, 8):
                    for column in range(0, columns, 128):
                        total = total + terms[start : start + 8, column : column + 128]
        rest[-1][...] = jnp.sum(total, axis=0, keepdims=True)


def finish_product(root, begun, factor, grad2, grad3, *others):
    slots, width, columns = grad2.shape
    out = jax.ShapeDtypeStruct(grad2.shape, BF16)
    shapes = (out, out) + ((jax.ShapeDtypeStruct((1, 128), F32),) if others else ())
    return call(
        finish_kernel,
        shapes,
        [IN_VMEM] * (5 + len(others)),
        (IN_VMEM,) * len(shapes),
        "near_product" if others else "far_product",
        flops=slots * 8 * width * width * columns,
        moved=slots * 16 * width * columns,
    )(root, begun, factor, grad3, grad2, *others)


def clip_kernel(slots, elements, plan_ref, *rest):
    sums, rows, out_hbm, out_ref, sems = rest[:4], rest[4:8], *rest[8:]
    plan = plan_ref[...]
    entry = lax.broadcasted_iota(jnp.int32, plan.shape, 1)
    blocks = [jnp.sum(jnp.where(entry == at, plan, 0)) for at in range(4 * slots)]
    lanes = sums[0][...] + sums[1][...] + sums[2][...] + sums[3][...]
    quadratic = jnp.sum(lanes, axis=1, keepdims=True)
    clip_factor = jnp.minimum(F32(1.0), jnp.sqrt(F32(KL_BOUND * elements) / quadratic))
    copies = []
    for far in range(4):
        for slot in range(slots):
            at = far * slots + slot
            out_ref[at] = (clip_factor * rows[far][slot].astype(F32)).astype(BF16)
            copies.append(
                pltpu.make_async_copy(out_ref.at[at], out_hbm.at[0, blocks[at]], sems.at[at])
            )
            copies[-1].start()
    for copy in copies:
        copy.wait()


def clip(plan, sums, rows, shape, slots, elements):
    return call(
        functools.partial(clip_kernel, slots, elements),
        jax.ShapeDtypeStruct(shape, BF16),
        [IN_VMEM] * (1 + len(sums) + len(rows)),
        ANYWHERE,
        "clip",
        scratch=[pltpu.VMEM(shape[1:], BF16), pltpu.SemaphoreType.DMA((shape[1],))],
        moved=4 * shape[1] * shape[2] * shape[3],
    )(plan[None], *sums, *rows)


def after_kernel(value_ref, landed_ref, out_ref):
    out_ref[...] = value_ref[...]


def after(value, landed):
    return call(
        after_kernel,
        jax.ShapeDtypeStruct(value.shape, value.dtype),
        [IN_VMEM, ANYWHERE],
        IN_VMEM,
        "after",
    )(value, landed)


def partner_of(value, axis, far):
    count = lax.axis_size(axis)
    return lax.ppermute(value, axis, [(i, i ^ far) for i in range(count)])


def sum_over(value, axis):
    count = lax.axis_size(axis)
    total = value
    for shift in range(1, count):
        total = total + lax.ppermute(
            value, axis, [(i, (i + shift) % count) for i in range(count)]
        )
    return total


def exchange_four(stats, grad, due, cost, assign, stale):
    slots = assign.shape[1] // 4
    me = lax.axis_index("fsdp").astype(jnp.int32)
    plan = plan_of(assign[0], me, slots)
    near, far2, far3 = pack_stats(me.reshape(1), assign, stats, slots)
    received = [partner_of(near, "fsdp", 1), partner_of(far3, "fsdp", 3), partner_of(far2, "fsdp", 2)]
    own_grad, *sent = pack_grad(plan, grad, slots)
    grad1, grad2, grad3 = [partner_of(piece, "fsdp", far) for far, piece in enumerate(sent, 1)]
    root, factor = roots(plan, due, cost, stats, received, stale, slots)
    far_root, near_root, far, near = start_product(plan, root, own_grad, grad1)
    out2, out3 = finish_product(far_root, far, factor, grad2, grad3)
    own, out1, total = finish_product(
        near_root, near, factor, grad2, grad3, own_grad, grad1, out2, out3
    )
    rows = [own] + [partner_of(out, "fsdp", far) for far, out in enumerate((out1, out2, out3), 1)]
    total = sum_over(total, "dp")
    sums = [total, partner_of(after(total, rows[3]), "fsdp", 1)]
    sums += [partner_of(total, "fsdp", far) for far in (2, 3)]
    elements = lax.axis_size("dp") * assign.shape[1] * stats.shape[3] * grad.shape[3]
    return clip(plan, sums, rows, grad.shape, slots, elements)


def solution(mesh):
    return jax.shard_map(
        exchange_four if mesh.shape["fsdp"] == 4 else exchange_all,
        mesh=mesh,
        in_specs=(
            P(("groups", "dp"), None, "fsdp", None),
            P(("groups", "dp"), None, "fsdp", None),
            P(("groups", "dp"), None),
            P(("groups", "dp"), None),
            P(("groups", "dp"), None),
            P(("groups", "dp"), "fsdp", None, None),
        ),
        out_specs=P(("groups", "dp"), None, "fsdp", None),
        check_vma=False,
    )
```
